32 devices in a mesh: chord: 4 (over y, x), wall: 8 (over z, core).
Axes of the slice: x: 2, y: 2, z: 4, core: 2. Of those that a mesh axis runs over, the one named last changes fastest.
Arguments:
- rhs: float32 [5, 16, 16, 512], P(None, None, 'wall', 'chord'), may hold values from -0.3 to 0.3
- jet_mask: int32 [16, 16, 512], P(None, 'wall', 'chord'), may hold values 0 or 1
- jet_source: float32 [5], replicated, may hold values from -0.3 to 0.3
- wall_flags: int32 [16, 512], P(None, 'chord'), may hold values from 0 to 2
- bc_table: float32 [3, 5], replicated, may hold values from 0.2 to 1.5
- xi_lower: float32 [5, 5, 16, 16, 512], P(None, None, None, 'wall', 'chord'), may hold values from -1.2 to 1.2
- xi_upper: float32 [5, 5, 16, 16, 512], P(None, None, None, 'wall', 'chord'), may hold values from -1.2 to 1.2
- eta_lower: float32 [5, 5, 16, 16, 512], P(None, None, None, 'wall', 'chord'), may hold values from -1.2 to 1.2
- eta_upper: float32 [5, 5, 16, 16, 512], P(None, None, None, 'wall', 'chord'), may hold values from -1.2 to 1.2
Outputs:
- increment: float32 [5, 16, 16, 512], P(None, None, 'wall', 'chord')
The draws below stay inside these ranges and needn't reach their ends.
All inputs are finite; a program needn't handle non-finite values. No bound on the sum of `jet_mask` on one device may be relied on, other than what follows from the above.
Results may differ from the reference program's by a relative error of at most 0.00019.
Values sent between devices are 32-bit elements; how exact they have to be, the bound alone decides.
A program may use at most 64 MiB of HBM per device.

```python
import math
import jax
import jax.numpy as jnp
from jax import lax

SPAN = 16
COMP = 5
FLAGS = 3
CHORD_CELLS = 512
NORMAL_CELLS = 16


def chain_blocks(key, pulse_length, chain_axis):
    random_keys = jax.random.split(key, 6)
    if chain_axis == 4:
        rate_shape = (5, SPAN, NORMAL_CELLS, 1)
        pulse_profile = (1, 1, 1, CHORD_CELLS)
    else:
        rate_shape = (5, SPAN, 1, CHORD_CELLS)
        pulse_profile = (1, 1, NORMAL_CELLS, 1)
    share_slow = 0.5
    slow = jax.random.uniform(random_keys[0], rate_shape) < share_slow
    slow_time = pulse_length * jnp.exp(jax.random.uniform(random_keys[1], rate_shape, minval=math.log(0.5), maxval=math.log(2.0)))
    fast_time = jax.random.uniform(random_keys[2], rate_shape, minval=30.0, maxval=50.0)
    pulse_rates = jnp.exp(-1.0 / jnp.where(slow, slow_time, fast_time))
    pulse_location = jax.random.uniform(random_keys[3], (pulse_length,)) < 3.0 / pulse_length
    pulse_threshold = jax.random.uniform(random_keys[4], (pulse_length,), minval=0.5, maxval=0.8)
    pulse_events = jnp.where(pulse_location, pulse_threshold, 1.0).reshape(pulse_profile)
    pulse_rates = pulse_rates * pulse_events
    raw = jax.random.uniform(random_keys[5], (5, 5, SPAN, NORMAL_CELLS, CHORD_CELLS), minval=-0.1, maxval=0.1)
    skew = raw - jnp.swapaxes(raw, 0, 1)
    frobenius = jnp.sum(skew * skew, axis=(0, 1))
    shrink = 1.0 / jnp.sqrt(1.0 + frobenius / 5.0)
    eye = jnp.eye(5, dtype=jnp.float32).reshape(5, 5, 1, 1, 1)
    blocks = pulse_rates[:, None] * (eye + skew) * shrink[None, None]
    return blocks.astype(jnp.float32)


def draw_xi_lower(key, part):
    return chain_blocks(jax.random.fold_in(key, 11), CHORD_CELLS, 4)


def draw_xi_upper(key, part):
    return chain_blocks(jax.random.fold_in(key, 12), CHORD_CELLS, 4)


def draw_eta_lower(key, part):
    return chain_blocks(jax.random.fold_in(key, 13), NORMAL_CELLS, 3)


def draw_eta_upper(key, part):
    return chain_blocks(jax.random.fold_in(key, 14), NORMAL_CELLS, 3)


def with_ends(values, stream_key, least, top_value):
    index_at = [jax.random.randint(jax.random.fold_in(stream_key, axis), (), 0, length) for axis, length in enumerate(values.shape)]
    widest = values.shape.index(max(values.shape))
    neighbour = index_at[:widest] + [(index_at[widest] + 1) % values.shape[widest]] + index_at[widest + 1:]
    return values.at[tuple(index_at)].set(least).at[tuple(neighbour)].set(top_value)


def block_scale(rng, shape, cuts, least, top_value):
    def one(position, parts):
        draws = jax.random.uniform(jax.random.fold_in(jax.random.fold_in(rng, 6), position), (parts,), jnp.float32, least / len(cuts), top_value / len(cuts))
        return jnp.repeat(jnp.exp(draws), shape[position] // parts).reshape((-1,) + (1,) * (len(shape) - position - 1))

    gain = one(*cuts[0])
    for cut in cuts[1:]:
        gain = gain * one(*cut)
    return gain


def bell_draw(rng, dims, scale, bound, pieces=(), kind=jnp.bfloat16):
    values = jax.random.normal(rng, dims, jnp.float32) * scale
    if len(pieces) > 0:
        values = block_scale(rng, dims, pieces, -0.22, 0.18) * values
    return jnp.clip(values, min=-bound, max=bound).astype(kind)


def setup_inputs(seed: int = 0) -> dict:
    splits = jax.random.split(jax.random.key(seed), 10)
    return {
        "rhs": bell_draw(splits[0], (COMP, SPAN, NORMAL_CELLS, CHORD_CELLS), 0.05, 0.3, ((2, 8), (3, 4)), jnp.float32),
        "jet_mask": with_ends((jax.random.randint(splits[1], (SPAN, NORMAL_CELLS, CHORD_CELLS), 0, 4) < 1).astype(jnp.int32), jax.random.fold_in(splits[1], 1), 0, 1),
        "jet_source": bell_draw(splits[2], (COMP,), 0.05, 0.3, (), jnp.float32),
        "wall_flags": with_ends(jax.random.randint(splits[3], (SPAN, CHORD_CELLS), 0, 3), jax.random.fold_in(splits[3], 1), 0, 2).astype(jnp.int32),
        "bc_table": jnp.clip(jax.random.uniform(splits[4], (FLAGS, COMP), jnp.float32, 0.2, 1.5), 0.2, 1.5),
        "xi_lower": draw_xi_lower(jax.random.fold_in(splits[9], 71), 0),
        "xi_upper": draw_xi_upper(jax.random.fold_in(splits[9], 71), 0),
        "eta_lower": draw_eta_lower(jax.random.fold_in(splits[9], 71), 0),
        "eta_upper": draw_eta_upper(jax.random.fold_in(splits[9], 71), 0),
    }


def run_chain(blocks, values, block_axis, reverse):
    value_axis = block_axis - 1
    blocks_first = jnp.moveaxis(blocks, block_axis, 0)
    values_first = jnp.moveaxis(values, value_axis, 0)

    def advance(carry, item):
        block, value = item
        fresh = jnp.einsum("ab...,b...->a...", block, carry, precision=lax.Precision.HIGHEST) + value
        return fresh, fresh

    start = jnp.zeros(values_first.shape[1:], jnp.float32)
    _, states = lax.scan(advance, start, (blocks_first, values_first), reverse=reverse)
    return jnp.moveaxis(states, 0, value_axis)


def reference(rhs, jet_mask, jet_source, wall_flags, bc_table, xi_lower, xi_upper, eta_lower, eta_upper):
    source = rhs + jet_mask.astype(jnp.float32)[None] * jet_source[:, None, None, None]
    ahead = run_chain(xi_lower, source, 4, False)
    behind = run_chain(xi_upper, ahead, 4, True)
    onehot = (wall_flags[None] == jnp.arange(FLAGS, dtype=jnp.int32)[:, None, None]).astype(jnp.float32)
    factor = jnp.einsum("fa,fki->aki", bc_table, onehot, precision=lax.Precision.HIGHEST)
    first_row = jnp.arange(NORMAL_CELLS, dtype=jnp.int32) == 0
    scaled = jnp.where(first_row[None, None, :, None], factor[:, :, None, :], jnp.float32(1.0)) * behind
    lifted = run_chain(eta_lower, scaled, 3, False)
    return run_chain(eta_upper, lifted, 3, True)
```

```python
import functools

import jax
import jax.numpy as jnp
from jax import lax
from jax.experimental import pallas as pl
from jax.experimental.pallas import tpu as pltpu
from jax.sharding import PartitionSpec as P

C = 5
ROWS = 8


def shifted(x, step, fill_eye, reverse):
    a, m, rows, width = x.shape
    flat = x.reshape(a * m * rows, width)
    moved = pltpu.roll(flat, width - step if reverse else step, 1).reshape(x.shape)
    lane = lax.broadcasted_iota(jnp.int32, x.shape, 3)
    keep = lane < width - step if reverse else lane >= step
    row = lax.broadcasted_iota(jnp.int32, x.shape, 0)
    col = lax.broadcasted_iota(jnp.int32, x.shape, 1)
    fill = jnp.where(row == col, 1.0, 0.0).astype(jnp.float32)
    return jnp.where(keep, moved, fill)


def apply_blocks(left, right):
    total = left[:, 0:1] * right[0:1]
    for b in range(1, C):
        total = total + left[:, b : b + 1] * right[b : b + 1]
    return total


def scan_lanes(blocks, values, reverse):
    both = jnp.concatenate([blocks, values], axis=1)
    step = 1
    while step < both.shape[3]:
        moved = shifted(both, step, True, reverse)
        made = apply_blocks(both[:, :C], moved)
        both = jnp.concatenate([made[:, :C], made[:, C:] + both[:, C:]], axis=1)
        step *= 2
    return both


def kernel(
    n_chord, n_wall, n_own,
    rhs_h, mask_h, jet, flags_v, table, xl_h, xu_h, el_h, eu_h,
    out_h,
    rhs, mask, xl, xu, el, eu, prefix, summary, sol, sol_in, res,
    load_sem, own_sem, chord_send, chord_recv, el_send, el_recv, eu_send, eu_recv,
    sol_send, sol_recv, res_send, res_recv,
):
    chord = lax.axis_index("chord")
    wall = lax.axis_index("wall")
    rows_per_owner = sol.shape[2]
    kpo = rows_per_owner // 2
    groups = rhs.shape[1] // ROWS
    width = rhs.shape[2]

    def when(own, cond_of):
        if n_own == n_wall:
            own()
        else:
            pl.when(cond_of)(own)

    loads = [
        pltpu.make_async_copy(h, v, load_sem.at[i])
        for i, (h, v) in enumerate(((rhs_h, rhs), (mask_h, mask), (xl_h, xl), (xu_h, xu)))
    ]
    for c in loads:
        c.start()

    barrier = pltpu.get_barrier_semaphore()
    for r in range(1, n_wall):
        pl.semaphore_signal(barrier, inc=1, device_id=(chord, lax.rem(wall + r, n_wall)),
                            device_id_type=pl.DeviceIdType.MESH)
    for r in range(1, n_chord):
        pl.semaphore_signal(barrier, inc=1, device_id=(lax.rem(chord + r, n_chord), wall),
                            device_id_type=pl.DeviceIdType.MESH)
    pl.semaphore_wait(barrier, n_wall + n_chord - 2)

    def to_wall(src, dst, send, recv, peer):
        return pltpu.make_async_remote_copy(
            src_ref=src, dst_ref=dst, send_sem=send, recv_sem=recv,
            device_id=(chord, peer), device_id_type=pl.DeviceIdType.MESH)

    for r in range(1, n_wall):
        peer = lax.rem(wall + r, n_wall)

        def send_eta(r=r, peer=peer):
            to_wall(el_h.at[:, peer], el.at[wall], el_send.at[r], el_recv.at[r], peer).start()
            to_wall(eu_h.at[:, peer], eu.at[wall], eu_send.at[r], eu_recv.at[r], peer).start()

        when(send_eta, peer < n_own)

    def own_eta():
        pltpu.make_async_copy(el_h.at[:, wall], el.at[wall], own_sem.at[0]).start()
        pltpu.make_async_copy(eu_h.at[:, wall], eu.at[wall], own_sem.at[1]).start()

    when(own_eta, wall < n_own)
    for c in loads:
        c.wait()

    lane = lax.broadcasted_iota(jnp.int32, (ROWS, width), 1)

    def chord_local(g, carry):
        at = pl.ds(pl.multiple_of(g * ROWS, ROWS), ROWS)
        hit = mask[at, :].astype(jnp.float32)
        source = jnp.stack([rhs[c, at, :] + hit * jet[c] for c in range(C)])[:, None]
        lower = scan_lanes(xl[:, at, :].reshape(C, C, ROWS, width), source, False)
        upper = scan_lanes(xu[:, at, :].reshape(C, C, ROWS, width), lower, True)
        prefix[:, at, :] = upper.reshape(C * 11, ROWS, width)
        packed = jnp.zeros((ROWS, width), jnp.float32)
        for a in range(C):
            for m in range(6):
                packed = jnp.where(lane == a * 6 + m, lower[a, m, :, width - 1 : width], packed)
            for m in range(11):
                packed = jnp.where(lane == 30 + a * 11 + m, upper[a, m, :, 0:1], packed)
        summary[chord, at, :] = packed
        return carry

    lax.fori_loop(0, groups, chord_local, 0)

    def to_chord(r, slot):
        return pltpu.make_async_remote_copy(
            src_ref=summary.at[slot], dst_ref=summary.at[slot],
            send_sem=chord_send.at[r], recv_sem=chord_recv.at[r],
            device_id=(lax.rem(chord + r, n_chord), wall), device_id_type=pl.DeviceIdType.MESH)

    for r in range(1, n_chord):
        to_chord(r, chord).start()
    for r in range(1, n_chord):
        to_chord(r, lax.rem(chord + n_chord - r, n_chord)).wait_recv()

    def chord_finish(g, carry):
        at = pl.ds(pl.multiple_of(g * ROWS, ROWS), ROWS)
        packs = [summary[d, at, :] for d in range(n_chord)]

        def field(d, i):
            return jnp.broadcast_to(packs[d][:, i : i + 1], (ROWS, width))

        zero = jnp.zeros((ROWS, width), jnp.float32)
        ins = [[zero] * C]
        for d in range(n_chord - 1):
            made = []
            for a in range(C):
                t = field(d, a * 6 + 5)
                if d > 0:
                    for b in range(C):
                        t = t + field(d, a * 6 + b) * ins[d][b]
                made.append(t)
            ins.append(made)
        backs = [None] * n_chord
        backs[n_chord - 1] = [zero] * C
        for d in range(n_chord - 1, 0, -1):
            made = []
            for a in range(C):
                base = 30 + a * 11
                t = field(d, base + 10)
                for b in range(C):
                    t = t + field(d, base + 5 + b) * ins[d][b]
                if d < n_chord - 1:
                    for b in range(C):
                        t = t + field(d, base + b) * backs[d][b]
                made.append(t)
            backs[d - 1] = made
        mine_in, mine_back = ins[0], backs[0]
        for d in range(1, n_chord):
            mine_in = [jnp.where(chord == d, x, y) for x, y in zip(ins[d], mine_in)]
            mine_back = [jnp.where(chord == d, x, y) for x, y in zip(backs[d], mine_back)]
        for a in range(C):
            t = prefix[a * 11 + 10, at, :]
            for b in range(C):
                t = t + prefix[a * 11 + 5 + b, at, :] * mine_in[b]
                t = t + prefix[a * 11 + b, at, :] * mine_back[b]
            for h in range(ROWS // rows_per_owner):
                sol[g * (ROWS // rows_per_owner) + h, a] = t[h * rows_per_owner : (h + 1) * rows_per_owner]
        return carry

    lax.fori_loop(0, groups, chord_finish, 0)

    for r in range(1, n_wall):
        peer = lax.rem(wall + r, n_wall)

        def send_sol(r=r, peer=peer):
            to_wall(sol.at[peer], sol_in.at[wall], sol_send.at[r], sol_recv.at[r], peer).start()

        when(send_sol, peer < n_own)

    def own_lines():
        own = pltpu.make_async_copy(sol.at[wall], sol_in.at[wall], own_sem.at[2])
        own.start()
        pltpu.make_async_copy(el_h.at[:, wall], el.at[wall], own_sem.at[0]).wait()
        pltpu.make_async_copy(eu_h.at[:, wall], eu.at[wall], own_sem.at[1]).wait()
        own.wait()
        for r in range(1, n_wall):
            source = lax.rem(wall + n_wall - r, n_wall)
            to_wall(el_h.at[:, 0], el.at[source], el_send.at[r], el_recv.at[r], source).wait_recv()
            to_wall(eu_h.at[:, 0], eu.at[source], eu_send.at[r], eu_recv.at[r], source).wait_recv()
            to_wall(sol.at[0], sol_in.at[source], sol_send.at[r], sol_recv.at[r], source).wait_recv()

        kind = flags_v[wall]
        factor = []
        for c in range(C):
            t = jnp.zeros(kind.shape, jnp.float32)
            for f in range(table.shape[0]):
                t = jnp.where(kind == f, table[f, c], t)
            factor.append(t)
        factor = jnp.stack(factor)

        def row(ref, d, j):
            return ref[d, :, pl.ds(j, kpo, stride=2), :]

        state = None
        lifted = []
        for d in range(n_wall):
            for j in range(2):
                value = row(sol_in, d, j)
                if state is None:
                    state = value * factor
                else:
                    blocks = row(el, d, j).reshape(C, C, kpo, width)
                    state = value + apply_blocks(blocks, state[:, None])[:, 0]
                lifted.append(state)
        state = None
        for d in range(n_wall - 1, -1, -1):
            for j in (1, 0):
                if state is None:
                    state = lifted[-1]
                else:
                    blocks = row(eu, d, j).reshape(C, C, kpo, width)
                    state = lifted[2 * d + j] + apply_blocks(blocks, state[:, None])[:, 0]
                res[d, :, pl.ds(j, kpo, stride=2), :] = state

        for r in range(1, n_wall):
            peer = lax.rem(wall + r, n_wall)
            to_wall(res.at[peer], out_h.at[:, wall], res_send.at[r], res_recv.at[r], peer).start()
        mine = pltpu.make_async_copy(res.at[wall], out_h.at[:, wall], own_sem.at[3])
        mine.start()
        mine.wait()
        for r in range(1, n_wall):
            peer = lax.rem(wall + r, n_wall)
            to_wall(res.at[peer], out_h.at[:, wall], res_send.at[r], res_recv.at[r], peer).wait_send()

    when(own_lines, wall < n_own)

    for r in range(1, n_wall):
        source = lax.rem(wall + n_wall - r, n_wall)
        peer = lax.rem(wall + r, n_wall)

        def take(r=r, source=source):
            to_wall(res.at[0], out_h.at[:, source], res_send.at[r], res_recv.at[r], source).wait_recv()

        def sent(r=r, peer=peer):
            to_wall(el_h.at[:, peer], el.at[wall], el_send.at[r], el_recv.at[r], peer).wait_send()
            to_wall(eu_h.at[:, peer], eu.at[wall], eu_send.at[r], eu_recv.at[r], peer).wait_send()
            to_wall(sol.at[peer], sol_in.at[wall], sol_send.at[r], sol_recv.at[r], peer).wait_send()

        when(take, source < n_own)
        when(sent, peer < n_own)
    for r in range(1, n_chord):
        to_chord(r, chord).wait_send()


def solution(mesh):
    n_chord, n_wall = mesh.shape["chord"], mesh.shape["wall"]

    def per_device(rhs, jet_mask, jet_source, wall_flags, bc_table,
                   xi_lower, xi_upper, eta_lower, eta_upper):
        comp, span, cells, width = rhs.shape
        n_own = min(n_wall, span)
        rows = span * cells
        rpo = rows // n_own
        flat = lambda x: x.reshape(comp * comp, rows, width)
        owned = lambda x: x.reshape(comp * comp, n_own, rpo, width)
        any_ = pl.BlockSpec(memory_space=pl.ANY)
        smem = pl.BlockSpec(memory_space=pltpu.SMEM)
        vmem = pl.BlockSpec(memory_space=pltpu.VMEM)
        f32 = jnp.float32
        dma = pltpu.SemaphoreType.DMA
        out = pl.pallas_call(
            functools.partial(kernel, n_chord, n_wall, n_own),
            out_shape=jax.ShapeDtypeStruct((comp, n_own, rpo, width), f32),
            in_specs=[any_, any_, smem, vmem, smem, any_, any_, any_, any_],
            out_specs=any_,
            scratch_shapes=[
                pltpu.VMEM((comp, rows, width), f32),
                pltpu.VMEM((rows, width), jnp.int32),
                pltpu.VMEM((comp * comp, rows, width), f32),
                pltpu.VMEM((comp * comp, rows, width), f32),
                pltpu.VMEM((n_wall, comp * comp, rpo, width), f32),
                pltpu.VMEM((n_wall, comp * comp, rpo, width), f32),
                pltpu.VMEM((comp * 11, rows, width), f32),
                pltpu.VMEM((n_chord, rows, width), f32),
                pltpu.VMEM((n_own, comp, rpo, width), f32),
                pltpu.VMEM((n_wall, comp, rpo, width), f32),
                pltpu.VMEM((n_wall, comp, rpo, width), f32),
                dma((4,)), dma((4,)), dma((n_chord,)), dma((n_chord,)),
                dma((n_wall,)), dma((n_wall,)), dma((n_wall,)), dma((n_wall,)),
                dma((n_wall,)), dma((n_wall,)), dma((n_wall,)), dma((n_wall,)),
            ],
            compiler_params=pltpu.CompilerParams(
                collective_id=0, has_side_effects=True, vmem_limit_bytes=48 * 1024 * 1024),
            name="sweeps",
        )(
            rhs.reshape(comp, rows, width), jet_mask.reshape(rows, width), jet_source,
            wall_flags.reshape(n_own, span // n_own, width), bc_table,
            flat(xi_lower), flat(xi_upper), owned(eta_lower), owned(eta_upper),
        )
        return out.reshape(comp, span, cells, width)

    placed = (
        P(None, None, "wall", "chord"),
        P(None, "wall", "chord"),
        P(),
        P(None, "chord"),
        P(),
        P(None, None, None, "wall", "chord"),
        P(None, None, None, "wall", "chord"),
        P(None, None, None, "wall", "chord"),
        P(None, None, None, "wall", "chord"),
    )
    return jax.shard_map(
        per_device, mesh=mesh, in_specs=placed,
        out_specs=P(None, None, "wall", "chord"), check_vma=False)
```

```python
import functools

import jax
import jax.numpy as jnp
from jax import lax
from jax.experimental import pallas as pl
from jax.experimental.pallas import tpu as pltpu
from jax.sharding import PartitionSpec as P

C = 5
ROWS = 8


def shifted(x, step, fill_eye, reverse):
    a, m, rows, width = x.shape
    flat = x.reshape(a * m * rows, width)
    moved = pltpu.roll(flat, width - step if reverse else step, 1).reshape(x.shape)
    lane = lax.broadcasted_iota(jnp.int32, x.shape, 3)
    keep = lane < width - step if reverse else lane >= step
    row = lax.broadcasted_iota(jnp.int32, x.shape, 0)
    col = lax.broadcasted_iota(jnp.int32, x.shape, 1)
    fill = jnp.where(row == col, 1.0, 0.0).astype(jnp.float32)
    return jnp.where(keep, moved, fill)


def apply_blocks(left, right):
    total = left[:, 0:1] * right[0:1]
    for b in range(1, C):
        total = total + left[:, b : b + 1] * right[b : b + 1]
    return total


def scan_lanes(blocks, values, reverse):
    both = jnp.concatenate([blocks, values], axis=1)
    step = 1
    while step < both.shape[3]:
        moved = shifted(both, step, True, reverse)
        made = apply_blocks(both[:, :C], moved)
        both = jnp.concatenate([made[:, :C], made[:, C:] + both[:, C:]], axis=1)
        step *= 2
    return both


def kernel(
    n_chord, n_wall, n_own,
    rhs_h, mask_h, jet_h, flags_h, table_h, xl_h, xu_h, el_h, eu_h,
    out_h,
    rhs, mask, xl, xu, jet, flags_v, table, el, eu, prefix, summary, sol, sol_in, res,
    load_sem, own_sem, chord_send, chord_recv, el_send, el_recv, eu_send, eu_recv,
    sol_send, sol_recv, res_send, res_recv,
):
    chord = lax.axis_index("chord")
    wall = lax.axis_index("wall")
    rows_per_owner = sol.shape[2]
    kpo = rows_per_owner // 2
    groups = rhs.shape[1] // ROWS
    width = rhs.shape[2]

    def when(own, cond_of):
        if n_own == n_wall:
            own()
        else:
            pl.when(cond_of)(own)

    loads = [
        pltpu.make_async_copy(h, v, load_sem.at[i])
        for i, (h, v) in enumerate(((xl_h, xl), (xu_h, xu), (rhs_h, rhs), (mask_h, mask),
                                   (jet_h, jet), (flags_h, flags_v), (table_h, table)))
    ]
    for c in loads:
        c.start()

    barrier = pltpu.get_barrier_semaphore()
    for r in range(1, n_wall):
        pl.semaphore_signal(barrier, inc=1, device_id=(chord, lax.rem(wall + r, n_wall)),
                            device_id_type=pl.DeviceIdType.MESH)
    for r in range(1, n_chord):
        pl.semaphore_signal(barrier, inc=1, device_id=(lax.rem(chord + r, n_chord), wall),
                            device_id_type=pl.DeviceIdType.MESH)
    pl.semaphore_wait(barrier, n_wall + n_chord - 2)

    def to_wall(src, dst, send, recv, peer):
        return pltpu.make_async_remote_copy(
            src_ref=src, dst_ref=dst, send_sem=send, recv_sem=recv,
            device_id=(chord, peer), device_id_type=pl.DeviceIdType.MESH)

    for r in range(1, n_wall):
        peer = lax.rem(wall + r, n_wall)

        def send_eta(r=r, peer=peer):
            to_wall(el_h.at[:, peer], el.at[wall], el_send.at[r], el_recv.at[r], peer).start()
            to_wall(eu_h.at[:, peer], eu.at[wall], eu_send.at[r], eu_recv.at[r], peer).start()

        when(send_eta, peer < n_own)

    def own_eta():
        pltpu.make_async_copy(el_h.at[:, wall], el.at[wall], own_sem.at[0]).start()
        pltpu.make_async_copy(eu_h.at[:, wall], eu.at[wall], own_sem.at[1]).start()

    when(own_eta, wall < n_own)
    for c in loads:
        c.wait()

    lane = lax.broadcasted_iota(jnp.int32, (ROWS, width), 1)

    def chord_local(g, carry):
        at = pl.ds(pl.multiple_of(g * ROWS, ROWS), ROWS)
        hit = mask[at, :].astype(jnp.float32)
        source = jnp.stack([rhs[c, at, :] + hit * jet[c] for c in range(C)])[:, None]
        lower = scan_lanes(xl[:, at, :].reshape(C, C, ROWS, width), source, False)
        upper = scan_lanes(xu[:, at, :].reshape(C, C, ROWS, width), lower, True)
        prefix[:, at, :] = upper.reshape(C * 11, ROWS, width)
        packed = jnp.zeros((ROWS, width), jnp.float32)
        for a in range(C):
            for m in range(6):
                packed = jnp.where(lane == a * 6 + m, lower[a, m, :, width - 1 : width], packed)
            for m in range(11):
                packed = jnp.where(lane == 30 + a * 11 + m, upper[a, m, :, 0:1], packed)
        summary[chord, at, :] = packed
        return carry

    lax.fori_loop(0, groups, chord_local, 0)

    def to_chord(r, slot):
        return pltpu.make_async_remote_copy(
            src_ref=summary.at[slot], dst_ref=summary.at[slot],
            send_sem=chord_send.at[r], recv_sem=chord_recv.at[r],
            device_id=(lax.rem(chord + r, n_chord), wall), device_id_type=pl.DeviceIdType.MESH)

    for r in range(1, n_chord):
        to_chord(r, chord).start()
    for r in range(1, n_chord):
        to_chord(r, lax.rem(chord + n_chord - r, n_chord)).wait_recv()

    def chord_finish(g, carry):
        at = pl.ds(pl.multiple_of(g * ROWS, ROWS), ROWS)
        packs = [summary[d, at, :] for d in range(n_chord)]

        def field(d, i):
            return jnp.broadcast_to(packs[d][:, i : i + 1], (ROWS, width))

        zero = jnp.zeros((ROWS, width), jnp.float32)
        ins = [[zero] * C]
        for d in range(n_chord - 1):
            made = []
            for a in range(C):
                t = field(d, a * 6 + 5)
                if d > 0:
                    for b in range(C):
                        t = t + field(d, a * 6 + b) * ins[d][b]
                made.append(t)
            ins.append(made)
        backs = [None] * n_chord
        backs[n_chord - 1] = [zero] * C
        for d in range(n_chord - 1, 0, -1):
            made = []
            for a in range(C):
                base = 30 + a * 11
                t = field(d, base + 10)
                for b in range(C):
                    t = t + field(d, base + 5 + b) * ins[d][b]
                if d < n_chord - 1:
                    for b in range(C):
                        t = t + field(d, base + b) * backs[d][b]
                made.append(t)
            backs[d - 1] = made
        mine_in, mine_back = ins[0], backs[0]
        for d in range(1, n_chord):
            mine_in = [jnp.where(chord == d, x, y) for x, y in zip(ins[d], mine_in)]
            mine_back = [jnp.where(chord == d, x, y) for x, y in zip(backs[d], mine_back)]
        for a in range(C):
            t = prefix[a * 11 + 10, at, :]
            for b in range(C):
                t = t + prefix[a * 11 + 5 + b, at, :] * mine_in[b]
                t = t + prefix[a * 11 + b, at, :] * mine_back[b]
            for h in range(ROWS // rows_per_owner):
                sol[g * (ROWS // rows_per_owner) + h, a] = t[h * rows_per_owner : (h + 1) * rows_per_owner]
        return carry

    lax.fori_loop(0, groups, chord_finish, 0)

    for r in range(1, n_wall):
        peer = lax.rem(wall + r, n_wall)

        def send_sol(r=r, peer=peer):
            to_wall(sol.at[peer], sol_in.at[wall], sol_send.at[r], sol_recv.at[r], peer).start()

        when(send_sol, peer < n_own)

    def own_lines():
        own = pltpu.make_async_copy(sol.at[wall], sol_in.at[wall], own_sem.at[2])
        own.start()
        pltpu.make_async_copy(el_h.at[:, wall], el.at[wall], own_sem.at[0]).wait()
        pltpu.make_async_copy(eu_h.at[:, wall], eu.at[wall], own_sem.at[1]).wait()
        own.wait()
        for r in range(1, n_wall):
            source = lax.rem(wall + n_wall - r, n_wall)
            to_wall(el_h.at[:, 0], el.at[source], el_send.at[r], el_recv.at[r], source).wait_recv()
            to_wall(eu_h.at[:, 0], eu.at[source], eu_send.at[r], eu_recv.at[r], source).wait_recv()
            to_wall(sol.at[0], sol_in.at[source], sol_send.at[r], sol_recv.at[r], source).wait_recv()

        kind = flags_v[wall]
        factor = []
        for c in range(C):
            t = jnp.zeros(kind.shape, jnp.float32)
            for f in range(table.shape[0]):
                t = jnp.where(kind == f, table[f, c], t)
            factor.append(t)
        factor = jnp.stack(factor)

        def row(ref, d, j):
            return ref[d, :, pl.ds(j, kpo, stride=2), :]

        state = None
        lifted = []
        for d in range(n_wall):
            for j in range(2):
                value = row(sol_in, d, j)
                if state is None:
                    state = value * factor
                else:
                    blocks = row(el, d, j).reshape(C, C, kpo, width)
                    state = value + apply_blocks(blocks, state[:, None])[:, 0]
                lifted.append(state)
        state = None
        for d in range(n_wall - 1, -1, -1):
            for j in (1, 0):
                if state is None:
                    state = lifted[-1]
                else:
                    blocks = row(eu, d, j).reshape(C, C, kpo, width)
                    state = lifted[2 * d + j] + apply_blocks(blocks, state[:, None])[:, 0]
                res[d, :, pl.ds(j, kpo, stride=2), :] = state

        for r in range(1, n_wall):
            peer = lax.rem(wall + r, n_wall)
            to_wall(res.at[peer], out_h.at[:, wall], res_send.at[r], res_recv.at[r], peer).start()
        mine = pltpu.make_async_copy(res.at[wall], out_h.at[:, wall], own_sem.at[3])
        mine.start()
        mine.wait()
        for r in range(1, n_wall):
            peer = lax.rem(wall + r, n_wall)
            to_wall(res.at[peer], out_h.at[:, wall], res_send.at[r], res_recv.at[r], peer).wait_send()

    when(own_lines, wall < n_own)

    for r in range(1, n_wall):
        source = lax.rem(wall + n_wall - r, n_wall)
        peer = lax.rem(wall + r, n_wall)

        def take(r=r, source=source):
            to_wall(res.at[0], out_h.at[:, source], res_send.at[r], res_recv.at[r], source).wait_recv()

        def sent(r=r, peer=peer):
            to_wall(el_h.at[:, peer], el.at[wall], el_send.at[r], el_recv.at[r], peer).wait_send()
            to_wall(eu_h.at[:, peer], eu.at[wall], eu_send.at[r], eu_recv.at[r], peer).wait_send()
            to_wall(sol.at[peer], sol_in.at[wall], sol_send.at[r], sol_recv.at[r], peer).wait_send()

        when(take, source < n_own)
        when(sent, peer < n_own)
    for r in range(1, n_chord):
        to_chord(r, chord).wait_send()


def solution(mesh):
    n_chord, n_wall = mesh.shape["chord"], mesh.shape["wall"]

    def per_device(rhs, jet_mask, jet_source, wall_flags, bc_table,
                   xi_lower, xi_upper, eta_lower, eta_upper):
        comp, span, cells, width = rhs.shape
        n_own = min(n_wall, span)
        rows = span * cells
        rpo = rows // n_own
        flat = lambda x: x.reshape(comp * comp, rows, width)
        owned = lambda x: x.reshape(comp * comp, n_own, rpo, width)
        hbm = pl.BlockSpec(memory_space=pltpu.HBM)
        f32 = jnp.float32
        dma = pltpu.SemaphoreType.DMA
        out = pl.pallas_call(
            functools.partial(kernel, n_chord, n_wall, n_own),
            out_shape=jax.ShapeDtypeStruct((comp, n_own, rpo, width), f32),
            in_specs=[hbm] * 9,
            out_specs=hbm,
            scratch_shapes=[
                pltpu.VMEM((comp, rows, width), f32),
                pltpu.VMEM((rows, width), jnp.int32),
                pltpu.VMEM((comp * comp, rows, width), f32),
                pltpu.VMEM((comp * comp, rows, width), f32),
                pltpu.SMEM(jet_source.shape, f32),
                pltpu.VMEM((n_own, span // n_own, width), jnp.int32),
                pltpu.SMEM(bc_table.shape, f32),
                pltpu.VMEM((n_wall, comp * comp, rpo, width), f32),
                pltpu.VMEM((n_wall, comp * comp, rpo, width), f32),
                pltpu.VMEM((comp * 11, rows, width), f32),
                pltpu.VMEM((n_chord, rows, width), f32),
                pltpu.VMEM((n_own, comp, rpo, width), f32),
                pltpu.VMEM((n_wall, comp, rpo, width), f32),
                pltpu.VMEM((n_wall, comp, rpo, width), f32),
                dma((7,)), dma((4,)), dma((n_chord,)), dma((n_chord,)),
                dma((n_wall,)), dma((n_wall,)), dma((n_wall,)), dma((n_wall,)),
                dma((n_wall,)), dma((n_wall,)), dma((n_wall,)), dma((n_wall,)),
            ],
            compiler_params=pltpu.CompilerParams(
                collective_id=0, has_side_effects=True, vmem_limit_bytes=64 * 1024 * 1024),
            name="sweeps",
        )(
            rhs.reshape(comp, rows, width), jet_mask.reshape(rows, width), jet_source,
            wall_flags.reshape(n_own, span // n_own, width), bc_table,
            flat(xi_lower), flat(xi_upper), owned(eta_lower), owned(eta_upper),
        )
        return out.reshape(comp, span, cells, width)

    placed = (
        P(None, None, "wall", "chord"),
        P(None, "wall", "chord"),
        P(),
        P(None, "chord"),
        P(),
        P(None, None, None, "wall", "chord"),
        P(None, None, None, "wall", "chord"),
        P(None, None, None, "wall", "chord"),
        P(None, None, None, "wall", "chord"),
    )
    return jax.shard_map(
        per_device, mesh=mesh, in_specs=placed,
        out_specs=P(None, None, "wall", "chord"), check_vma=False)
```

```python
import functools

import jax
import jax.numpy as jnp
from jax import lax
from jax.experimental import pallas as pl
from jax.experimental.pallas import tpu as pltpu
from jax.sharding import PartitionSpec as P

C = 5
ROWS = 8


def shifted(x, step, fill_eye, reverse):
    a, m, rows, width = x.shape
    flat = x.reshape(a * m * rows, width)
    moved = pltpu.roll(flat, width - step if reverse else step, 1).reshape(x.shape)
    lane = lax.broadcasted_iota(jnp.int32, x.shape, 3)
    keep = lane < width - step if reverse else lane >= step
    row = lax.broadcasted_iota(jnp.int32, x.shape, 0)
    col = lax.broadcasted_iota(jnp.int32, x.shape, 1)
    fill = jnp.where(row == col, 1.0, 0.0).astype(jnp.float32)
    return jnp.where(keep, moved, fill)


def apply_blocks(left, right):
    total = left[:, 0:1] * right[0:1]
    for b in range(1, C):
        total = total + left[:, b : b + 1] * right[b : b + 1]
    return total


def scan_lanes(blocks, values, reverse):
    both = jnp.concatenate([blocks, values], axis=1)
    step = 1
    while step < both.shape[3]:
        moved = shifted(both, step, True, reverse)
        made = apply_blocks(both[:, :C], moved)
        both = jnp.concatenate([made[:, :C], made[:, C:] + both[:, C:]], axis=1)
        step *= 2
    return both


def kernel(
    n_chord, n_z, n_zo,
    rhs_h, mask_h, jet_h, flags_h, table_h, xl_h, xu_h, el_h, eu_h,
    out_h,
    rhs, mask, xl, xu, jet, flags_v, table, el, eu, prefix, summary, sol, sol_in, res,
    maps_out, maps_in, ends_out, ends_in, flow_out, flow_in, flow,
    load_sem, own_sem, chord_send, chord_recv, pair_send, pair_recv,
    maps_send, maps_recv, ends_send, ends_recv, flow_send, flow_recv,
):
    chord = lax.axis_index("chord")
    wall = lax.axis_index("wall")
    zi, core = wall // 2, lax.rem(wall, 2)
    other = 1 - core
    groups = rhs.shape[1] // ROWS
    half_groups = groups // 2
    lines = el.shape[2] // 2
    width = rhs.shape[2]
    kz = maps_out.shape[2]

    def when(own, cond_of):
        if n_zo == n_z:
            own()
        else:
            pl.when(cond_of)(own)

    loads = [
        pltpu.make_async_copy(h, v, load_sem.at[i])
        for i, (h, v) in enumerate(((xl_h, xl), (xu_h, xu), (rhs_h, rhs), (mask_h, mask),
                                   (jet_h, jet), (flags_h, flags_v), (table_h, table)))
    ]
    for c in loads:
        c.start()

    barrier = pltpu.get_barrier_semaphore()
    pl.semaphore_signal(barrier, inc=1, device_id=(chord, zi * 2 + other),
                        device_id_type=pl.DeviceIdType.MESH)
    for r in range(1, n_z):
        pl.semaphore_signal(barrier, inc=1, device_id=(chord, lax.rem(zi + r, n_z) * 2 + core),
                            device_id_type=pl.DeviceIdType.MESH)
    for r in range(1, n_chord):
        pl.semaphore_signal(barrier, inc=1, device_id=(lax.rem(chord + r, n_chord), wall),
                            device_id_type=pl.DeviceIdType.MESH)
    pl.semaphore_wait(barrier, n_z + n_chord - 1)

    def to_wall(src, dst, send, recv, peer):
        return pltpu.make_async_remote_copy(
            src_ref=src, dst_ref=dst, send_sem=send, recv_sem=recv,
            device_id=(chord, peer), device_id_type=pl.DeviceIdType.MESH)

    def to_core(i, src, dst):
        return to_wall(src, dst, pair_send.at[i], pair_recv.at[i], zi * 2 + other)

    def to_z(src, dst, send, recv, z):
        return to_wall(src, dst, send, recv, z * 2 + core)

    to_core(0, el_h.at[:, other], el.at[core]).start()
    to_core(1, eu_h.at[:, other], eu.at[core]).start()
    own_el = pltpu.make_async_copy(el_h.at[:, core], el.at[core], own_sem.at[0])
    own_eu = pltpu.make_async_copy(eu_h.at[:, core], eu.at[core], own_sem.at[1])
    own_el.start()
    own_eu.start()
    for c in loads:
        c.wait()

    def cell(ref, j):
        return ref[j // 2, :, pl.ds(j % 2, lines, stride=2), :]

    def block(ref, j):
        return cell(ref, j).reshape(C, C, lines, width)

    lane = lax.broadcasted_iota(jnp.int32, (ROWS, width), 1)

    def chord_local(g, carry):
        at = pl.ds(pl.multiple_of(g * ROWS, ROWS), ROWS)
        hit = mask[at, :].astype(jnp.float32)
        source = jnp.stack([rhs[c, at, :] + hit * jet[c] for c in range(C)])[:, None]
        lower = scan_lanes(xl[:, at, :].reshape(C, C, ROWS, width), source, False)
        upper = scan_lanes(xu[:, at, :].reshape(C, C, ROWS, width), lower, True)
        prefix[:, at, :] = upper.reshape(C * 11, ROWS, width)
        packed = jnp.zeros((ROWS, width), jnp.float32)
        for a in range(C):
            for m in range(6):
                packed = jnp.where(lane == a * 6 + m, lower[a, m, :, width - 1 : width], packed)
            for m in range(11):
                packed = jnp.where(lane == 30 + a * 11 + m, upper[a, m, :, 0:1], packed)
        summary[chord, at, :] = packed
        return carry

    lax.fori_loop(0, half_groups, chord_local, 0)

    own_el.wait()
    own_eu.wait()
    to_core(0, el_h.at[:, 0], el.at[other]).wait_recv()
    to_core(1, eu_h.at[:, 0], eu.at[other]).wait_recv()
    reach = [block(el, 0)]
    for j in range(1, 4):
        reach.append(apply_blocks(block(el, j), reach[-1]))
    back, through = reach[3], block(eu, 3)
    for j in (2, 1, 0):
        blocks = block(eu, j)
        back = apply_blocks(blocks, back) + reach[j]
        through = apply_blocks(blocks, through)
    for i, m in enumerate((reach[3], back, through)):
        m = m.reshape(C * C, lines, width)
        for o in range(n_zo):
            maps_out[o, i * 25 : (i + 1) * 25] = m[:, o * kz : (o + 1) * kz]

    def scatter(src, dst, send, recv):
        for r in range(1, n_z):
            z = lax.rem(zi + r, n_z)
            when(lambda r=r, z=z: to_z(src.at[z], dst.at[zi], send.at[r], recv.at[r], z).start(), z < n_zo)

    def scatter_own(src, dst, sem):
        return pltpu.make_async_copy(src.at[zi], dst.at[zi], sem)

    def scatter_sent(src, dst, send, recv):
        for r in range(1, n_z):
            z = lax.rem(zi + r, n_z)
            when(lambda r=r, z=z: to_z(src.at[z], dst.at[zi], send.at[r], recv.at[r], z).wait_send(), z < n_zo)

    def scattered(src, dst, send, recv):
        for r in range(1, n_z):
            z = lax.rem(zi + n_z - r, n_z)
            to_z(src.at[0], dst.at[z], send.at[r], recv.at[r], z).wait_recv()

    owner = zi < n_zo
    scatter(maps_out, maps_in, maps_send, maps_recv)
    when(lambda: scatter_own(maps_out, maps_in, own_sem.at[2]).start(), owner)
    lax.fori_loop(half_groups, groups, chord_local, 0)

    def to_chord(r, slot):
        return pltpu.make_async_remote_copy(
            src_ref=summary.at[slot], dst_ref=summary.at[slot],
            send_sem=chord_send.at[r], recv_sem=chord_recv.at[r],
            device_id=(lax.rem(chord + r, n_chord), wall), device_id_type=pl.DeviceIdType.MESH)

    for r in range(1, n_chord):
        to_chord(r, chord).start()
    for r in range(1, n_chord):
        to_chord(r, lax.rem(chord + n_chord - r, n_chord)).wait_recv()

    def chord_finish(g, carry):
        at = pl.ds(pl.multiple_of(g * ROWS, ROWS), ROWS)
        packs = [summary[d, at, :] for d in range(n_chord)]

        def field(d, i):
            return jnp.broadcast_to(packs[d][:, i : i + 1], (ROWS, width))

        zero = jnp.zeros((ROWS, width), jnp.float32)
        ins = [[zero] * C]
        for d in range(n_chord - 1):
            made = []
            for a in range(C):
                t = field(d, a * 6 + 5)
                if d > 0:
                    for b in range(C):
                        t = t + field(d, a * 6 + b) * ins[d][b]
                made.append(t)
            ins.append(made)
        backs = [None] * n_chord
        backs[n_chord - 1] = [zero] * C
        for d in range(n_chord - 1, 0, -1):
            made = []
            for a in range(C):
                base = 30 + a * 11
                t = field(d, base + 10)
                for b in range(C):
                    t = t + field(d, base + 5 + b) * ins[d][b]
                if d < n_chord - 1:
                    for b in range(C):
                        t = t + field(d, base + b) * backs[d][b]
                made.append(t)
            backs[d - 1] = made
        mine_in, mine_back = ins[0], backs[0]
        for d in range(1, n_chord):
            mine_in = [jnp.where(chord == d, x, y) for x, y in zip(ins[d], mine_in)]
            mine_back = [jnp.where(chord == d, x, y) for x, y in zip(backs[d], mine_back)]
        for a in range(C):
            t = prefix[a * 11 + 10, at, :]
            for b in range(C):
                t = t + prefix[a * 11 + 5 + b, at, :] * mine_in[b]
                t = t + prefix[a * 11 + b, at, :] * mine_back[b]
            sol[g // half_groups, a,
                pl.ds(pl.multiple_of(lax.rem(g, half_groups) * ROWS, ROWS), ROWS), :] = t
        return carry

    lax.fori_loop(0, groups, chord_finish, 0)

    to_core(2, sol.at[other], sol_in.at[core]).start()
    own_sol = pltpu.make_async_copy(sol.at[core], sol_in.at[core], own_sem.at[3])
    own_sol.start()
    kind = flags_v[core]
    factor = []
    for c in range(C):
        t = jnp.zeros(kind.shape, jnp.float32)
        for f in range(table.shape[0]):
            t = jnp.where(kind == f, table[f, c], t)
        factor.append(jnp.where(zi == 0, t, 1.0))
    factor = jnp.stack(factor)
    own_sol.wait()
    to_core(2, sol.at[0], sol_in.at[other]).wait_recv()

    def value(j):
        return cell(sol_in, j) * factor if j == 0 else cell(sol_in, j)

    def step(ref, j, state):
        return apply_blocks(block(ref, j), state[:, None])[:, 0]

    lifted = [value(0)]
    for j in range(1, 4):
        lifted.append(value(j) + step(el, j, lifted[-1]))
    first = lifted[3]
    for j in (2, 1, 0):
        first = lifted[j] + step(eu, j, first)
    for o in range(n_zo):
        ends_out[o, :C] = lifted[3][:, o * kz : (o + 1) * kz]
        ends_out[o, C:] = first[:, o * kz : (o + 1) * kz]
    scatter(ends_out, ends_in, ends_send, ends_recv)
    when(lambda: scatter_own(ends_out, ends_in, own_sem.at[4]).start(), owner)

    def own_lines():
        scatter_own(maps_out, maps_in, own_sem.at[2]).wait()
        scattered(maps_out, maps_in, maps_send, maps_recv)
        scatter_own(ends_out, ends_in, own_sem.at[4]).wait()
        scattered(ends_out, ends_in, ends_send, ends_recv)

        def through_map(z, i, state):
            m = maps_in[z, i * 25 : (i + 1) * 25].reshape(C, C, kz, width)
            return apply_blocks(m, state[:, None])[:, 0]

        zero = jnp.zeros((C, kz, width), jnp.float32)
        ins = [zero, ends_in[0, :C]]
        for z in range(1, n_z - 1):
            ins.append(ends_in[z, :C] + through_map(z, 0, ins[-1]))
        backs = [zero]
        for z in range(n_z - 1, 0, -1):
            t = ends_in[z, C:] + through_map(z, 1, ins[z])
            if z < n_z - 1:
                t = t + through_map(z, 2, backs[-1])
            backs.append(t)
        backs = backs[::-1]
        for z in range(n_z):
            flow_out[z, :C] = ins[z]
            flow_out[z, C:] = backs[z]
        for r in range(1, n_z):
            z = lax.rem(zi + r, n_z)
            to_z(flow_out.at[z], flow_in.at[zi], flow_send.at[r], flow_recv.at[r], z).start()
        scatter_own(flow_out, flow_in, own_sem.at[5]).start()

    when(own_lines, owner)
    when(lambda: scatter_own(flow_out, flow_in, own_sem.at[5]).wait(), owner)
    for r in range(1, n_z):
        z = lax.rem(zi + n_z - r, n_z)
        when(lambda r=r, z=z: to_z(flow_out.at[0], flow_in.at[z], flow_send.at[r], flow_recv.at[r], z).wait_recv(),
             z < n_zo)
    for o in range(n_zo):
        flow[:, o * kz : (o + 1) * kz] = flow_in[o]

    def ship(half):
        @pl.when(core == half)
        def _():
            pltpu.make_async_copy(res.at[half], out_h.at[:, half], own_sem.at[6]).start()

        @pl.when(core != half)
        def _():
            to_core(3, res.at[half], out_h.at[:, core]).start()

    state = flow[:C]
    lifted = []
    for j in range(4):
        state = value(j) + step(el, j, state)
        lifted.append(state)
    state = flow[C:]
    for j in (3, 2, 1, 0):
        state = lifted[j] + step(eu, j, state)
        res[j // 2, :, pl.ds(j % 2, lines, stride=2), :] = state
        if j % 2 == 0:
            ship(j // 2)

    for i, src, dst in ((0, el_h.at[:, other], el.at[core]), (1, eu_h.at[:, other], eu.at[core]),
                        (2, sol.at[other], sol_in.at[core]), (3, res.at[other], out_h.at[:, core])):
        to_core(i, src, dst).wait_send()
    scatter_sent(maps_out, maps_in, maps_send, maps_recv)
    scatter_sent(ends_out, ends_in, ends_send, ends_recv)

    def flow_sent():
        for r in range(1, n_z):
            z = lax.rem(zi + r, n_z)
            to_z(flow_out.at[z], flow_in.at[zi], flow_send.at[r], flow_recv.at[r], z).wait_send()

    when(flow_sent, owner)
    for r in range(1, n_chord):
        to_chord(r, chord).wait_send()
    pltpu.make_async_copy(res.at[core], out_h.at[:, core], own_sem.at[6]).wait()
    to_core(3, res.at[0], out_h.at[:, other]).wait_recv()


def solution(mesh):
    n_chord, n_wall = mesh.shape["chord"], mesh.shape["wall"]

    def per_device(rhs, jet_mask, jet_source, wall_flags, bc_table,
                   xi_lower, xi_upper, eta_lower, eta_upper):
        comp, span, cells, width = rhs.shape
        n_z = n_wall // 2
        lines = span // 2
        n_zo = min(n_z, lines)
        kz = lines // n_zo
        rows = span * cells
        half = rows // 2
        flat = lambda x: x.reshape(comp * comp, rows, width)
        halved = lambda x: x.reshape(comp * comp, 2, half, width)
        hbm = pl.BlockSpec(memory_space=pltpu.HBM)
        f32 = jnp.float32
        dma = pltpu.SemaphoreType.DMA
        out = pl.pallas_call(
            functools.partial(kernel, n_chord, n_z, n_zo),
            out_shape=jax.ShapeDtypeStruct((comp, 2, half, width), f32),
            in_specs=[hbm] * 9,
            out_specs=hbm,
            scratch_shapes=[
                pltpu.VMEM((comp, rows, width), f32),
                pltpu.VMEM((rows, width), jnp.int32),
                pltpu.VMEM((comp * comp, rows, width), f32),
                pltpu.VMEM((comp * comp, rows, width), f32),
                pltpu.SMEM(jet_source.shape, f32),
                pltpu.VMEM((2, lines, width), jnp.int32),
                pltpu.SMEM(bc_table.shape, f32),
                pltpu.VMEM((2, comp * comp, half, width), f32),
                pltpu.VMEM((2, comp * comp, half, width), f32),
                pltpu.VMEM((comp * 11, rows, width), f32),
                pltpu.VMEM((n_chord, rows, width), f32),
                pltpu.VMEM((2, comp, half, width), f32),
                pltpu.VMEM((2, comp, half, width), f32),
                pltpu.VMEM((2, comp, half, width), f32),
                pltpu.VMEM((n_zo, 3 * comp * comp, kz, width), f32),
                pltpu.VMEM((n_z, 3 * comp * comp, kz, width), f32),
                pltpu.VMEM((n_zo, 2 * comp, kz, width), f32),
                pltpu.VMEM((n_z, 2 * comp, kz, width), f32),
                pltpu.VMEM((n_z, 2 * comp, kz, width), f32),
                pltpu.VMEM((n_zo, 2 * comp, kz, width), f32),
                pltpu.VMEM((2 * comp, lines, width), f32),
                dma((7,)), dma((7,)), dma((n_chord,)), dma((n_chord,)), dma((4,)), dma((4,)),
                dma((n_z,)), dma((n_z,)), dma((n_z,)), dma((n_z,)), dma((n_z,)), dma((n_z,)),
            ],
            compiler_params=pltpu.CompilerParams(
                collective_id=0, has_side_effects=True, vmem_limit_bytes=64 * 1024 * 1024),
            name="sweeps",
        )(
            rhs.reshape(comp, rows, width), jet_mask.reshape(rows, width), jet_source,
            wall_flags.reshape(2, lines, width), bc_table,
            flat(xi_lower), flat(xi_upper), halved(eta_lower), halved(eta_upper),
        )
        return out.reshape(comp, span, cells, width)

    placed = (
        P(None, None, "wall", "chord"),
        P(None, "wall", "chord"),
        P(),
        P(None, "chord"),
        P(),
        P(None, None, None, "wall", "chord"),
        P(None, None, None, "wall", "chord"),
        P(None, None, None, "wall", "chord"),
        P(None, None, None, "wall", "chord"),
    )
    return jax.shard_map(
        per_device, mesh=mesh, in_specs=placed,
        out_specs=P(None, None, "wall", "chord"), check_vma=False)
```

```python
import functools

import jax
import jax.numpy as jnp
from jax import lax
from jax.experimental import pallas as pl
from jax.experimental.pallas import tpu as pltpu
from jax.sharding import PartitionSpec as P

C = 5
ROWS = 8
PACK = 4


def shifted(x, step, fill_eye, reverse):
    a, m, rows, width = x.shape
    flat = x.reshape(a * m * rows, width)
    moved = pltpu.roll(flat, width - step if reverse else step, 1).reshape(x.shape)
    lane = lax.broadcasted_iota(jnp.int32, x.shape, 3)
    keep = lane < width - step if reverse else lane >= step
    row = lax.broadcasted_iota(jnp.int32, x.shape, 0)
    col = lax.broadcasted_iota(jnp.int32, x.shape, 1)
    fill = jnp.where(row == col, 1.0, 0.0).astype(jnp.float32)
    return jnp.where(keep, moved, fill)


def apply_blocks(left, right):
    total = left[:, 0:1] * right[0:1]
    for b in range(1, C):
        total = total + left[:, b : b + 1] * right[b : b + 1]
    return total


def compose(later, earlier):
    made = apply_blocks(later[:, :C], earlier)
    return jnp.concatenate([made[:, :C], made[:, C:] + later[:, C:]], axis=1)


def scan_lanes(both, reverse):
    step = PACK
    while step < both.shape[3]:
        both = compose(both, shifted(both, step, True, reverse))
        step *= 2
    return both


def roll2(x, by):
    width = x.shape[-1]
    return pltpu.roll(x.reshape(-1, width), by % width, 1).reshape(x.shape)


def interleave(parts):
    lane = lax.broadcasted_iota(jnp.int32, parts[0].shape, 2)
    for bit in (1, 2):
        odd = (lane & bit) != 0
        made = list(parts)
        for i in range(PACK):
            if i & bit == 0:
                lo, hi = parts[i], parts[i | bit]
                made[i] = jnp.where(odd, roll2(hi, bit), lo)
                made[i | bit] = jnp.where(odd, hi, roll2(lo, -bit))
        parts = made
    return parts


def kernel(
    n_chord, n_z, n_zo,
    rhs_h, mask_h, jet_h, flags_h, table_h, xl_h, xu_h, el_h, eu_h,
    out_h,
    rhs, mask, xl, xu, jet, flags_v, table, el, eu, prefix, summary, sol, sol_in, res,
    maps_out, maps_in, ends_out, ends_in, flow_out, flow_in, flow,
    load_sem, own_sem, chord_send, chord_recv, pair_send, pair_recv,
    maps_send, maps_recv, ends_send, ends_recv, flow_send, flow_recv,
):
    chord = lax.axis_index("chord")
    wall = lax.axis_index("wall")
    zi, core = wall // 2, lax.rem(wall, 2)
    other = 1 - core
    groups = rhs.shape[1] // ROWS
    half_groups = groups // 2
    lines = el.shape[2] // 2
    width = rhs.shape[2]
    kz = maps_out.shape[2]

    def when(own, cond_of):
        if n_zo == n_z:
            own()
        else:
            pl.when(cond_of)(own)

    loads = [
        pltpu.make_async_copy(h, v, load_sem.at[i])
        for i, (h, v) in enumerate(((xl_h, xl), (xu_h, xu), (rhs_h, rhs), (mask_h, mask),
                                   (jet_h, jet), (flags_h, flags_v), (table_h, table)))
    ]
    for c in loads:
        c.start()

    barrier = pltpu.get_barrier_semaphore()
    pl.semaphore_signal(barrier, inc=1, device_id=(chord, zi * 2 + other),
                        device_id_type=pl.DeviceIdType.MESH)
    for r in range(1, n_z):
        pl.semaphore_signal(barrier, inc=1, device_id=(chord, lax.rem(zi + r, n_z) * 2 + core),
                            device_id_type=pl.DeviceIdType.MESH)
    for r in range(1, n_chord):
        pl.semaphore_signal(barrier, inc=1, device_id=(lax.rem(chord + r, n_chord), wall),
                            device_id_type=pl.DeviceIdType.MESH)
    pl.semaphore_wait(barrier, n_z + n_chord - 1)

    def to_wall(src, dst, send, recv, peer):
        return pltpu.make_async_remote_copy(
            src_ref=src, dst_ref=dst, send_sem=send, recv_sem=recv,
            device_id=(chord, peer), device_id_type=pl.DeviceIdType.MESH)

    def to_core(i, src, dst):
        return to_wall(src, dst, pair_send.at[i], pair_recv.at[i], zi * 2 + other)

    def to_z(src, dst, send, recv, z):
        return to_wall(src, dst, send, recv, z * 2 + core)

    to_core(0, el_h.at[:, other], el.at[core]).start()
    to_core(1, eu_h.at[:, other], eu.at[core]).start()
    own_el = pltpu.make_async_copy(el_h.at[:, core], el.at[core], own_sem.at[0])
    own_eu = pltpu.make_async_copy(eu_h.at[:, core], eu.at[core], own_sem.at[1])
    own_el.start()
    own_eu.start()
    for c in loads:
        c.wait()

    def cell(ref, j):
        return ref[j // 2, :, pl.ds(j % 2, lines, stride=2), :]

    def block(ref, j):
        return cell(ref, j).reshape(C, C, lines, width)

    lane = lax.broadcasted_iota(jnp.int32, (ROWS, width), 1)

    def tile(ref, q):
        return ref[:, q * ROWS : (q + 1) * ROWS, :]

    def sources(q):
        hit = mask[q * ROWS : (q + 1) * ROWS, :].astype(jnp.float32)
        x = tile(rhs, q)
        return jnp.stack([x[c] + hit * jet[c] for c in range(C)])

    source = interleave([sources(q) for q in range(PACK)])
    lower = interleave([tile(xl, q) for q in range(PACK)])
    runs = []
    for t in range(PACK):
        x = jnp.concatenate([lower[t].reshape(C, C, ROWS, width), source[t][:, None]], axis=1)
        runs.append(compose(x, runs[-1]) if runs else x)
    last = scan_lanes(runs[PACK - 1], False)
    before = shifted(last, PACK, True, False)
    full = [compose(runs[t], before) for t in range(PACK - 1)] + [last]
    upper = interleave([tile(xu, q) for q in range(PACK)])
    runs = [None] * PACK
    for t in range(PACK - 1, -1, -1):
        x = jnp.concatenate([upper[t].reshape(C, C, ROWS, width), full[t]], axis=1)
        runs[t] = compose(x, runs[t + 1]) if t < PACK - 1 else x
    first = scan_lanes(runs[0], True)
    before = shifted(first, PACK, True, True)
    packs = [jnp.zeros((ROWS, width), jnp.float32) for _ in range(summary.shape[1])]
    fields = [(last[a, m], PACK - width) for a in range(C) for m in range(6)]
    fields += [(first[a, m], 0) for a in range(C) for m in range(11)]
    per = width // PACK
    for i, (x, base) in enumerate(fields):
        at = PACK * (i % per)
        packs[i // per] = jnp.where((lane >= at) & (lane < at + PACK), roll2(x, at + base), packs[i // per])
    for i, x in enumerate(packs):
        summary[chord, i] = x

    def to_chord(r, slot):
        return pltpu.make_async_remote_copy(
            src_ref=summary.at[slot], dst_ref=summary.at[slot],
            send_sem=chord_send.at[r], recv_sem=chord_recv.at[r],
            device_id=(lax.rem(chord + r, n_chord), wall), device_id_type=pl.DeviceIdType.MESH)

    for r in range(1, n_chord):
        to_chord(r, chord).start()
    prefix[0] = first.reshape(C * 11, ROWS, width)
    for t in range(1, PACK):
        prefix[t] = compose(runs[t], before).reshape(C * 11, ROWS, width)

    own_el.wait()
    own_eu.wait()
    to_core(0, el_h.at[:, 0], el.at[other]).wait_recv()
    to_core(1, eu_h.at[:, 0], eu.at[other]).wait_recv()
    reach = [block(el, 0)]
    for j in range(1, 4):
        reach.append(apply_blocks(block(el, j), reach[-1]))
    back, through = reach[3], block(eu, 3)
    for j in (2, 1, 0):
        blocks = block(eu, j)
        back = apply_blocks(blocks, back) + reach[j]
        through = apply_blocks(blocks, through)
    for i, m in enumerate((reach[3], back, through)):
        m = m.reshape(C * C, lines, width)
        for o in range(n_zo):
            maps_out[o, i * 25 : (i + 1) * 25] = m[:, o * kz : (o + 1) * kz]

    def scatter(src, dst, send, recv):
        for r in range(1, n_z):
            z = lax.rem(zi + r, n_z)
            when(lambda r=r, z=z: to_z(src.at[z], dst.at[zi], send.at[r], recv.at[r], z).start(), z < n_zo)

    def scatter_own(src, dst, sem):
        return pltpu.make_async_copy(src.at[zi], dst.at[zi], sem)

    def scatter_sent(src, dst, send, recv):
        for r in range(1, n_z):
            z = lax.rem(zi + r, n_z)
            when(lambda r=r, z=z: to_z(src.at[z], dst.at[zi], send.at[r], recv.at[r], z).wait_send(), z < n_zo)

    def scattered(src, dst, send, recv):
        for r in range(1, n_z):
            z = lax.rem(zi + n_z - r, n_z)
            to_z(src.at[0], dst.at[z], send.at[r], recv.at[r], z).wait_recv()

    owner = zi < n_zo
    scatter(maps_out, maps_in, maps_send, maps_recv)
    when(lambda: scatter_own(maps_out, maps_in, own_sem.at[2]).start(), owner)
    for r in range(1, n_chord):
        to_chord(r, lax.rem(chord + n_chord - r, n_chord)).wait_recv()


    def field(d, i):
        return roll2(summary[d, i // per], -PACK * (i % per))

    zero = jnp.zeros((ROWS, width), jnp.float32)
    ins = [[zero] * C]
    for d in range(n_chord - 1):
        made = []
        for a in range(C):
            t = field(d, a * 6 + 5)
            if d > 0:
                for b in range(C):
                    t = t + field(d, a * 6 + b) * ins[d][b]
            made.append(t)
        ins.append(made)
    backs = [None] * n_chord
    backs[n_chord - 1] = [zero] * C
    for d in range(n_chord - 1, 0, -1):
        made = []
        for a in range(C):
            base = 30 + a * 11
            t = field(d, base + 10)
            for b in range(C):
                t = t + field(d, base + 5 + b) * ins[d][b]
            if d < n_chord - 1:
                for b in range(C):
                    t = t + field(d, base + b) * backs[d][b]
            made.append(t)
        backs[d - 1] = made
    mine_in, mine_back = ins[0], backs[0]
    for d in range(1, n_chord):
        mine_in = [jnp.where(chord == d, x, y) for x, y in zip(ins[d], mine_in)]
        mine_back = [jnp.where(chord == d, x, y) for x, y in zip(backs[d], mine_back)]
    inflow = jnp.where(lane[None] < PACK, jnp.stack(mine_in + mine_back), 0.0)
    by = PACK
    while by < width:
        inflow = inflow + roll2(inflow, by)
        by *= 2
    behind = []
    for t in range(PACK):
        x = prefix[t].reshape(C, 11, ROWS, width)
        total = x[:, 10]
        for b in range(C):
            total = total + x[:, 5 + b] * inflow[b] + x[:, b] * inflow[C + b]
        behind.append(total)
    for q, x in enumerate(interleave(behind)):
        at = (q % half_groups) * ROWS
        sol[q // half_groups, :, at : at + ROWS, :] = x

    to_core(2, sol.at[other], sol_in.at[core]).start()
    own_sol = pltpu.make_async_copy(sol.at[core], sol_in.at[core], own_sem.at[3])
    own_sol.start()
    kind = flags_v[core]
    factor = []
    for c in range(C):
        t = jnp.zeros(kind.shape, jnp.float32)
        for f in range(table.shape[0]):
            t = jnp.where(kind == f, table[f, c], t)
        factor.append(jnp.where(zi == 0, t, 1.0))
    factor = jnp.stack(factor)
    own_sol.wait()
    to_core(2, sol.at[0], sol_in.at[other]).wait_recv()

    def value(j):
        return cell(sol_in, j) * factor if j == 0 else cell(sol_in, j)

    def step(ref, j, state):
        return apply_blocks(block(ref, j), state[:, None])[:, 0]

    lifted = [value(0)]
    for j in range(1, 4):
        lifted.append(value(j) + step(el, j, lifted[-1]))
    first = lifted[3]
    for j in (2, 1, 0):
        first = lifted[j] + step(eu, j, first)
    for o in range(n_zo):
        ends_out[o, :C] = lifted[3][:, o * kz : (o + 1) * kz]
        ends_out[o, C:] = first[:, o * kz : (o + 1) * kz]
    scatter(ends_out, ends_in, ends_send, ends_recv)
    when(lambda: scatter_own(ends_out, ends_in, own_sem.at[4]).start(), owner)

    def own_lines():
        scatter_own(maps_out, maps_in, own_sem.at[2]).wait()
        scattered(maps_out, maps_in, maps_send, maps_recv)
        scatter_own(ends_out, ends_in, own_sem.at[4]).wait()
        scattered(ends_out, ends_in, ends_send, ends_recv)

        def through_map(z, i, state):
            m = maps_in[z, i * 25 : (i + 1) * 25].reshape(C, C, kz, width)
            return apply_blocks(m, state[:, None])[:, 0]

        zero = jnp.zeros((C, kz, width), jnp.float32)
        ins = [zero, ends_in[0, :C]]
        for z in range(1, n_z - 1):
            ins.append(ends_in[z, :C] + through_map(z, 0, ins[-1]))
        backs = [zero]
        for z in range(n_z - 1, 0, -1):
            t = ends_in[z, C:] + through_map(z, 1, ins[z])
            if z < n_z - 1:
                t = t + through_map(z, 2, backs[-1])
            backs.append(t)
        backs = backs[::-1]
        for z in range(n_z):
            flow_out[z, :C] = ins[z]
            flow_out[z, C:] = backs[z]
        for r in range(1, n_z):
            z = lax.rem(zi + r, n_z)
            to_z(flow_out.at[z], flow_in.at[zi], flow_send.at[r], flow_recv.at[r], z).start()
        scatter_own(flow_out, flow_in, own_sem.at[5]).start()

    when(own_lines, owner)
    when(lambda: scatter_own(flow_out, flow_in, own_sem.at[5]).wait(), owner)
    for r in range(1, n_z):
        z = lax.rem(zi + n_z - r, n_z)
        when(lambda r=r, z=z: to_z(flow_out.at[0], flow_in.at[z], flow_send.at[r], flow_recv.at[r], z).wait_recv(),
             z < n_zo)
    for o in range(n_zo):
        flow[:, o * kz : (o + 1) * kz] = flow_in[o]

    def ship(half):
        @pl.when(core == half)
        def _():
            pltpu.make_async_copy(res.at[half], out_h.at[:, half], own_sem.at[6]).start()

        @pl.when(core != half)
        def _():
            to_core(3, res.at[half], out_h.at[:, core]).start()

    state = flow[:C]
    lifted = []
    for j in range(4):
        state = value(j) + step(el, j, state)
        lifted.append(state)
    state = flow[C:]
    for j in (3, 2, 1, 0):
        state = lifted[j] + step(eu, j, state)
        res[j // 2, :, pl.ds(j % 2, lines, stride=2), :] = state
        if j % 2 == 0:
            ship(j // 2)

    for i, src, dst in ((0, el_h.at[:, other], el.at[core]), (1, eu_h.at[:, other], eu.at[core]),
                        (2, sol.at[other], sol_in.at[core]), (3, res.at[other], out_h.at[:, core])):
        to_core(i, src, dst).wait_send()
    scatter_sent(maps_out, maps_in, maps_send, maps_recv)
    scatter_sent(ends_out, ends_in, ends_send, ends_recv)

    def flow_sent():
        for r in range(1, n_z):
            z = lax.rem(zi + r, n_z)
            to_z(flow_out.at[z], flow_in.at[zi], flow_send.at[r], flow_recv.at[r], z).wait_send()

    when(flow_sent, owner)
    for r in range(1, n_chord):
        to_chord(r, chord).wait_send()
    pltpu.make_async_copy(res.at[core], out_h.at[:, core], own_sem.at[6]).wait()
    to_core(3, res.at[0], out_h.at[:, other]).wait_recv()


def solution(mesh):
    n_chord, n_wall = mesh.shape["chord"], mesh.shape["wall"]

    def per_device(rhs, jet_mask, jet_source, wall_flags, bc_table,
                   xi_lower, xi_upper, eta_lower, eta_upper):
        comp, span, cells, width = rhs.shape
        n_z = n_wall // 2
        lines = span // 2
        n_zo = min(n_z, lines)
        kz = lines // n_zo
        rows = span * cells
        half = rows // 2
        flat = lambda x: x.reshape(comp * comp, rows, width)
        halved = lambda x: x.reshape(comp * comp, 2, half, width)
        hbm = pl.BlockSpec(memory_space=pltpu.HBM)
        f32 = jnp.float32
        dma = pltpu.SemaphoreType.DMA
        out = pl.pallas_call(
            functools.partial(kernel, n_chord, n_z, n_zo),
            out_shape=jax.ShapeDtypeStruct((comp, 2, half, width), f32),
            in_specs=[hbm] * 9,
            out_specs=hbm,
            scratch_shapes=[
                pltpu.VMEM((comp, rows, width), f32),
                pltpu.VMEM((rows, width), jnp.int32),
                pltpu.VMEM((comp * comp, rows, width), f32),
                pltpu.VMEM((comp * comp, rows, width), f32),
                pltpu.SMEM(jet_source.shape, f32),
                pltpu.VMEM((2, lines, width), jnp.int32),
                pltpu.SMEM(bc_table.shape, f32),
                pltpu.VMEM((2, comp * comp, half, width), f32),
                pltpu.VMEM((2, comp * comp, half, width), f32),
                pltpu.VMEM((PACK, comp * 11, ROWS, width), f32),
                pltpu.VMEM((n_chord, -(-85 * PACK // width), ROWS, width), f32),
                pltpu.VMEM((2, comp, half, width), f32),
                pltpu.VMEM((2, comp, half, width), f32),
                pltpu.VMEM((2, comp, half, width), f32),
                pltpu.VMEM((n_zo, 3 * comp * comp, kz, width), f32),
                pltpu.VMEM((n_z, 3 * comp * comp, kz, width), f32),
                pltpu.VMEM((n_zo, 2 * comp, kz, width), f32),
                pltpu.VMEM((n_z, 2 * comp, kz, width), f32),
                pltpu.VMEM((n_z, 2 * comp, kz, width), f32),
                pltpu.VMEM((n_zo, 2 * comp, kz, width), f32),
                pltpu.VMEM((2 * comp, lines, width), f32),
                dma((7,)), dma((7,)), dma((n_chord,)), dma((n_chord,)), dma((4,)), dma((4,)),
                dma((n_z,)), dma((n_z,)), dma((n_z,)), dma((n_z,)), dma((n_z,)), dma((n_z,)),
            ],
            compiler_params=pltpu.CompilerParams(
                collective_id=0, has_side_effects=True, vmem_limit_bytes=64 * 1024 * 1024),
            name="sweeps",
        )(
            rhs.reshape(comp, rows, width), jet_mask.reshape(rows, width), jet_source,
            wall_flags.reshape(2, lines, width), bc_table,
            flat(xi_lower), flat(xi_upper), halved(eta_lower), halved(eta_upper),
        )
        return out.reshape(comp, span, cells, width)

    placed = (
        P(None, None, "wall", "chord"),
        P(None, "wall", "chord"),
        P(),
        P(None, "chord"),
        P(),
        P(None, None, None, "wall", "chord"),
        P(None, None, None, "wall", "chord"),
        P(None, None, None, "wall", "chord"),
        P(None, None, None, "wall", "chord"),
    )
    return jax.shard_map(
        per_device, mesh=mesh, in_specs=placed,
        out_specs=P(None, None, "wall", "chord"), check_vma=False)
```

```python
import functools

import jax
import jax.numpy as jnp
from jax import lax
from jax.experimental import pallas as pl
from jax.experimental.pallas import tpu as pltpu
from jax.sharding import PartitionSpec as P

C = 5
ROWS = 8
PACK = 4


def shifted(x, step, fill_eye, reverse):
    a, m, rows, width = x.shape
    flat = x.reshape(a * m * rows, width)
    moved = pltpu.roll(flat, width - step if reverse else step, 1).reshape(x.shape)
    lane = lax.broadcasted_iota(jnp.int32, x.shape, 3)
    keep = lane < width - step if reverse else lane >= step
    row = lax.broadcasted_iota(jnp.int32, x.shape, 0)
    col = lax.broadcasted_iota(jnp.int32, x.shape, 1)
    fill = jnp.where(row == col, 1.0, 0.0).astype(jnp.float32)
    return jnp.where(keep, moved, fill)


def apply_blocks(left, right):
    total = left[:, 0:1] * right[0:1]
    for b in range(1, C):
        total = total + left[:, b : b + 1] * right[b : b + 1]
    return total


def compose(later, earlier):
    made = apply_blocks(later[:, :C], earlier)
    return jnp.concatenate([made[:, :C], made[:, C:] + later[:, C:]], axis=1)


def scan_lanes(both, reverse):
    step = PACK
    while step < both.shape[3]:
        both = compose(both, shifted(both, step, True, reverse))
        step *= 2
    return both


def roll2(x, by):
    width = x.shape[-1]
    return pltpu.roll(x.reshape(-1, width), by % width, 1).reshape(x.shape)


def interleave(parts):
    lane = lax.broadcasted_iota(jnp.int32, parts[0].shape, 2)
    for bit in (1, 2):
        odd = (lane & bit) != 0
        made = list(parts)
        for i in range(PACK):
            if i & bit == 0:
                lo, hi = parts[i], parts[i | bit]
                made[i] = jnp.where(odd, roll2(hi, bit), lo)
                made[i | bit] = jnp.where(odd, hi, roll2(lo, -bit))
        parts = made
    return parts


def kernel(
    n_chord, n_z, n_zo,
    rhs_h, mask_h, jet_h, flags_h, table_h, xl_h, xu_h, el_h, eu_h,
    out_h,
    rhs, mask, xl, xu, jet, flags_v, table, el, eu, prefix, summary, sol, sol_in, res,
    maps_out, maps_in, ends_out, ends_in, flow_out, flow_in, flow,
    load_sem, own_sem, chord_send, chord_recv, pair_send, pair_recv,
    maps_send, maps_recv, ends_send, ends_recv, flow_send, flow_recv,
):
    chord = lax.axis_index("chord")
    wall = lax.axis_index("wall")
    zi, core = wall // 2, lax.rem(wall, 2)
    other = 1 - core
    groups = rhs.shape[1] // ROWS
    half_groups = groups // 2
    lines = el.shape[2] // 2
    width = rhs.shape[2]
    kz = maps_out.shape[2]

    def when(own, cond_of):
        if n_zo == n_z:
            own()
        else:
            pl.when(cond_of)(own)

    loads = [
        pltpu.make_async_copy(h, v, load_sem.at[i])
        for i, (h, v) in enumerate(((xl_h, xl), (xu_h, xu), (rhs_h, rhs), (mask_h, mask),
                                   (jet_h, jet), (flags_h, flags_v), (table_h, table)))
    ]
    for c in loads:
        c.start()

    barrier = pltpu.get_barrier_semaphore()
    pl.semaphore_signal(barrier, inc=1, device_id=(chord, zi * 2 + other),
                        device_id_type=pl.DeviceIdType.MESH)
    for r in range(1, n_z):
        pl.semaphore_signal(barrier, inc=1, device_id=(chord, lax.rem(zi + r, n_z) * 2 + core),
                            device_id_type=pl.DeviceIdType.MESH)
    for r in range(1, n_chord):
        pl.semaphore_signal(barrier, inc=1, device_id=(lax.rem(chord + r, n_chord), wall),
                            device_id_type=pl.DeviceIdType.MESH)
    pl.semaphore_wait(barrier, n_z + n_chord - 1)

    def to_wall(src, dst, send, recv, peer):
        return pltpu.make_async_remote_copy(
            src_ref=src, dst_ref=dst, send_sem=send, recv_sem=recv,
            device_id=(chord, peer), device_id_type=pl.DeviceIdType.MESH)

    def to_core(i, src, dst):
        return to_wall(src, dst, pair_send.at[i], pair_recv.at[i], zi * 2 + other)

    def to_z(src, dst, send, recv, z):
        return to_wall(src, dst, send, recv, z * 2 + core)

    to_core(0, el_h.at[:, other], el.at[core]).start()
    to_core(1, eu_h.at[:, other], eu.at[core]).start()
    own_el = pltpu.make_async_copy(el_h.at[:, core], el.at[core], own_sem.at[0])
    own_eu = pltpu.make_async_copy(eu_h.at[:, core], eu.at[core], own_sem.at[1])
    own_el.start()
    own_eu.start()
    for i in (0, 2, 3, 4):
        loads[i].wait()

    def cell(ref, j):
        return ref[j // 2, :, pl.ds(j % 2, lines, stride=2), :]

    def block(ref, j):
        return cell(ref, j).reshape(C, C, lines, width)

    lane = lax.broadcasted_iota(jnp.int32, (ROWS, width), 1)

    def tile(ref, q):
        return ref[:, q * ROWS : (q + 1) * ROWS, :]

    def sources(q):
        hit = mask[q * ROWS : (q + 1) * ROWS, :].astype(jnp.float32)
        x = tile(rhs, q)
        return jnp.stack([x[c] + hit * jet[c] for c in range(C)])

    source = interleave([sources(q) for q in range(PACK)])
    lower = interleave([tile(xl, q) for q in range(PACK)])
    runs = []
    for t in range(PACK):
        x = jnp.concatenate([lower[t].reshape(C, C, ROWS, width), source[t][:, None]], axis=1)
        runs.append(compose(x, runs[-1]) if runs else x)
    last = scan_lanes(runs[PACK - 1], False)
    before = shifted(last, PACK, True, False)
    full = [compose(runs[t], before) for t in range(PACK - 1)] + [last]
    loads[1].wait()
    upper = interleave([tile(xu, q) for q in range(PACK)])
    runs = [None] * PACK
    for t in range(PACK - 1, -1, -1):
        x = jnp.concatenate([upper[t].reshape(C, C, ROWS, width), full[t]], axis=1)
        runs[t] = compose(x, runs[t + 1]) if t < PACK - 1 else x
    first = scan_lanes(runs[0], True)
    before = shifted(first, PACK, True, True)
    packs = [jnp.zeros((ROWS, width), jnp.float32) for _ in range(summary.shape[1])]
    fields = [(last[a, m], PACK - width) for a in range(C) for m in range(6)]
    fields += [(first[a, m], 0) for a in range(C) for m in range(11)]
    per = width // PACK
    for i, (x, base) in enumerate(fields):
        at = PACK * (i % per)
        packs[i // per] = jnp.where((lane >= at) & (lane < at + PACK), roll2(x, at + base), packs[i // per])
    for i, x in enumerate(packs):
        summary[chord, i] = x

    def to_chord(r, slot):
        return pltpu.make_async_remote_copy(
            src_ref=summary.at[slot], dst_ref=summary.at[slot],
            send_sem=chord_send.at[r], recv_sem=chord_recv.at[r],
            device_id=(lax.rem(chord + r, n_chord), wall), device_id_type=pl.DeviceIdType.MESH)

    for r in range(1, n_chord):
        to_chord(r, chord).start()
    prefix[0] = first.reshape(C * 11, ROWS, width)
    for t in range(1, PACK):
        prefix[t] = compose(runs[t], before).reshape(C * 11, ROWS, width)

    own_el.wait()
    own_eu.wait()
    to_core(0, el_h.at[:, 0], el.at[other]).wait_recv()
    to_core(1, eu_h.at[:, 0], eu.at[other]).wait_recv()
    reach = [block(el, 0)]
    for j in range(1, 4):
        reach.append(apply_blocks(block(el, j), reach[-1]))
    back, through = reach[3], block(eu, 3)
    for j in (2, 1, 0):
        blocks = block(eu, j)
        back = apply_blocks(blocks, back) + reach[j]
        through = apply_blocks(blocks, through)
    for i, m in enumerate((back, reach[3], through)):
        m = m.reshape(C * C, lines, width)
        for o in range(n_zo):
            maps_out[o, i * 25 : (i + 1) * 25] = m[:, o * kz : (o + 1) * kz]

    def scatter(src, dst, send, recv):
        for r in range(1, n_z):
            z = lax.rem(zi + r, n_z)
            when(lambda r=r, z=z: to_z(src.at[z], dst.at[zi], send.at[r], recv.at[r], z).start(), z < n_zo)

    def scatter_own(src, dst, sem):
        return pltpu.make_async_copy(src.at[zi], dst.at[zi], sem)

    def scatter_sent(src, dst, send, recv):
        for r in range(1, n_z):
            z = lax.rem(zi + r, n_z)
            when(lambda r=r, z=z: to_z(src.at[z], dst.at[zi], send.at[r], recv.at[r], z).wait_send(), z < n_zo)

    def scattered(src, dst, send, recv):
        for r in range(1, n_z):
            z = lax.rem(zi + n_z - r, n_z)
            to_z(src.at[0], dst.at[z], send.at[r], recv.at[r], z).wait_recv()

    owner = zi < n_zo
    def map_copies(z_out, z_in, r, to):
        return [
            to_z(maps_out.at[z_out, part], maps_in.at[z_in, part], maps_send.at[i, r], maps_recv.at[i, r], to)
            for i, part in enumerate((pl.ds(0, C * C), pl.ds(C * C, 2 * C * C)))
        ]

    def each_map(act, copies, sender, condition):
        turn, inner = sender > 0, (sender > 0) & (sender < n_z - 1)
        if condition is not None:
            turn, inner = turn & condition, inner & condition
        pl.when(turn)(lambda: act(copies[0]))
        pl.when(inner)(lambda: act(copies[1]))

    def maps_outward(act):
        for r in range(1, n_z):
            z = lax.rem(zi + r, n_z)
            each_map(act, map_copies(z, zi, r, z), zi, None if n_zo == n_z else z < n_zo)

    maps_outward(lambda c: c.start())
    when(lambda: scatter_own(maps_out, maps_in, own_sem.at[2]).start(), owner)
    for r in range(1, n_chord):
        to_chord(r, lax.rem(chord + n_chord - r, n_chord)).wait_recv()


    def field(d, i):
        return roll2(summary[d, i // per], -PACK * (i % per))

    zero = jnp.zeros((ROWS, width), jnp.float32)
    ins = [[zero] * C]
    for d in range(n_chord - 1):
        made = []
        for a in range(C):
            t = field(d, a * 6 + 5)
            if d > 0:
                for b in range(C):
                    t = t + field(d, a * 6 + b) * ins[d][b]
            made.append(t)
        ins.append(made)
    backs = [None] * n_chord
    backs[n_chord - 1] = [zero] * C
    for d in range(n_chord - 1, 0, -1):
        made = []
        for a in range(C):
            base = 30 + a * 11
            t = field(d, base + 10)
            for b in range(C):
                t = t + field(d, base + 5 + b) * ins[d][b]
            if d < n_chord - 1:
                for b in range(C):
                    t = t + field(d, base + b) * backs[d][b]
            made.append(t)
        backs[d - 1] = made
    mine_in, mine_back = ins[0], backs[0]
    for d in range(1, n_chord):
        mine_in = [jnp.where(chord == d, x, y) for x, y in zip(ins[d], mine_in)]
        mine_back = [jnp.where(chord == d, x, y) for x, y in zip(backs[d], mine_back)]
    inflow = jnp.where(lane[None] < PACK, jnp.stack(mine_in + mine_back), 0.0)
    by = PACK
    while by < width:
        inflow = inflow + roll2(inflow, by)
        by *= 2
    behind = []
    for t in range(PACK):
        x = prefix[t].reshape(C, 11, ROWS, width)
        total = x[:, 10]
        for b in range(C):
            total = total + x[:, 5 + b] * inflow[b] + x[:, b] * inflow[C + b]
        behind.append(total)
    for q, x in enumerate(interleave(behind)):
        at = (q % half_groups) * ROWS
        sol[q // half_groups, :, at : at + ROWS, :] = x

    to_core(2, sol.at[other], sol_in.at[core]).start()
    own_sol = pltpu.make_async_copy(sol.at[core], sol_in.at[core], own_sem.at[3])
    own_sol.start()
    loads[5].wait()
    loads[6].wait()
    kind = flags_v[core]
    factor = []
    for c in range(C):
        t = jnp.zeros(kind.shape, jnp.float32)
        for f in range(table.shape[0]):
            t = jnp.where(kind == f, table[f, c], t)
        factor.append(jnp.where(zi == 0, t, 1.0))
    factor = jnp.stack(factor)
    own_sol.wait()
    to_core(2, sol.at[0], sol_in.at[other]).wait_recv()

    def value(j):
        return cell(sol_in, j) * factor if j == 0 else cell(sol_in, j)

    def step(ref, j, state):
        return apply_blocks(block(ref, j), state[:, None])[:, 0]

    lifted = [value(0)]
    for j in range(1, 4):
        lifted.append(value(j) + step(el, j, lifted[-1]))
    first = lifted[3]
    for j in (2, 1, 0):
        first = lifted[j] + step(eu, j, first)
    for o in range(n_zo):
        ends_out[o, :C] = lifted[3][:, o * kz : (o + 1) * kz]
        ends_out[o, C:] = first[:, o * kz : (o + 1) * kz]
    scatter(ends_out, ends_in, ends_send, ends_recv)
    when(lambda: scatter_own(ends_out, ends_in, own_sem.at[4]).start(), owner)

    def own_lines():
        scatter_own(maps_out, maps_in, own_sem.at[2]).wait()
        for r in range(1, n_z):
            z = lax.rem(zi + n_z - r, n_z)
            each_map(lambda c: c.wait_recv(), map_copies(0, z, r, z), z, None)
        scatter_own(ends_out, ends_in, own_sem.at[4]).wait()
        scattered(ends_out, ends_in, ends_send, ends_recv)

        def through_map(z, i, state):
            m = maps_in[z, i * 25 : (i + 1) * 25].reshape(C, C, kz, width)
            return apply_blocks(m, state[:, None])[:, 0]

        zero = jnp.zeros((C, kz, width), jnp.float32)
        ins = [zero, ends_in[0, :C]]
        for z in range(1, n_z - 1):
            ins.append(ends_in[z, :C] + through_map(z, 1, ins[-1]))
        backs = [zero]
        for z in range(n_z - 1, 0, -1):
            t = ends_in[z, C:] + through_map(z, 0, ins[z])
            if z < n_z - 1:
                t = t + through_map(z, 2, backs[-1])
            backs.append(t)
        backs = backs[::-1]
        for z in range(n_z):
            flow_out[z, :C] = ins[z]
            flow_out[z, C:] = backs[z]
        for r in range(1, n_z):
            z = lax.rem(zi + r, n_z)
            to_z(flow_out.at[z], flow_in.at[zi], flow_send.at[r], flow_recv.at[r], z).start()
        scatter_own(flow_out, flow_in, own_sem.at[5]).start()

    when(own_lines, owner)
    when(lambda: scatter_own(flow_out, flow_in, own_sem.at[5]).wait(), owner)
    for r in range(1, n_z):
        z = lax.rem(zi + n_z - r, n_z)
        when(lambda r=r, z=z: to_z(flow_out.at[0], flow_in.at[z], flow_send.at[r], flow_recv.at[r], z).wait_recv(),
             z < n_zo)
    for o in range(n_zo):
        flow[:, o * kz : (o + 1) * kz] = flow_in[o]

    def ship(half):
        @pl.when(core == half)
        def _():
            pltpu.make_async_copy(res.at[half], out_h.at[:, half], own_sem.at[6]).start()

        @pl.when(core != half)
        def _():
            to_core(3, res.at[half], out_h.at[:, core]).start()

    state = flow[:C]
    lifted = []
    for j in range(4):
        state = value(j) + step(el, j, state)
        lifted.append(state)
    state = flow[C:]
    for j in (3, 2, 1, 0):
        state = lifted[j] + step(eu, j, state)
        res[j // 2, :, pl.ds(j % 2, lines, stride=2), :] = state
        if j % 2 == 0:
            ship(j // 2)

    for i, src, dst in ((0, el_h.at[:, other], el.at[core]), (1, eu_h.at[:, other], eu.at[core]),
                        (2, sol.at[other], sol_in.at[core]), (3, res.at[other], out_h.at[:, core])):
        to_core(i, src, dst).wait_send()
    maps_outward(lambda c: c.wait_send())
    scatter_sent(ends_out, ends_in, ends_send, ends_recv)

    def flow_sent():
        for r in range(1, n_z):
            z = lax.rem(zi + r, n_z)
            to_z(flow_out.at[z], flow_in.at[zi], flow_send.at[r], flow_recv.at[r], z).wait_send()

    when(flow_sent, owner)
    for r in range(1, n_chord):
        to_chord(r, chord).wait_send()
    pltpu.make_async_copy(res.at[core], out_h.at[:, core], own_sem.at[6]).wait()
    to_core(3, res.at[0], out_h.at[:, other]).wait_recv()


def solution(mesh):
    n_chord, n_wall = mesh.shape["chord"], mesh.shape["wall"]

    def per_device(rhs, jet_mask, jet_source, wall_flags, bc_table,
                   xi_lower, xi_upper, eta_lower, eta_upper):
        comp, span, cells, width = rhs.shape
        n_z = n_wall // 2
        lines = span // 2
        n_zo = min(n_z, lines)
        kz = lines // n_zo
        rows = span * cells
        half = rows // 2
        flat = lambda x: x.reshape(comp * comp, rows, width)
        halved = lambda x: x.reshape(comp * comp, 2, half, width)
        hbm = pl.BlockSpec(memory_space=pltpu.HBM)
        f32 = jnp.float32
        dma = pltpu.SemaphoreType.DMA
        out = pl.pallas_call(
            functools.partial(kernel, n_chord, n_z, n_zo),
            out_shape=jax.ShapeDtypeStruct((comp, 2, half, width), f32),
            in_specs=[hbm] * 9,
            out_specs=hbm,
            scratch_shapes=[
                pltpu.VMEM((comp, rows, width), f32),
                pltpu.VMEM((rows, width), jnp.int32),
                pltpu.VMEM((comp * comp, rows, width), f32),
                pltpu.VMEM((comp * comp, rows, width), f32),
                pltpu.SMEM(jet_source.shape, f32),
                pltpu.VMEM((2, lines, width), jnp.int32),
                pltpu.SMEM(bc_table.shape, f32),
                pltpu.VMEM((2, comp * comp, half, width), f32),
                pltpu.VMEM((2, comp * comp, half, width), f32),
                pltpu.VMEM((PACK, comp * 11, ROWS, width), f32),
                pltpu.VMEM((n_chord, -(-85 * PACK // width), ROWS, width), f32),
                pltpu.VMEM((2, comp, half, width), f32),
                pltpu.VMEM((2, comp, half, width), f32),
                pltpu.VMEM((2, comp, half, width), f32),
                pltpu.VMEM((n_zo, 3 * comp * comp, kz, width), f32),
                pltpu.VMEM((n_z, 3 * comp * comp, kz, width), f32),
                pltpu.VMEM((n_zo, 2 * comp, kz, width), f32),
                pltpu.VMEM((n_z, 2 * comp, kz, width), f32),
                pltpu.VMEM((n_z, 2 * comp, kz, width), f32),
                pltpu.VMEM((n_zo, 2 * comp, kz, width), f32),
                pltpu.VMEM((2 * comp, lines, width), f32),
                dma((7,)), dma((7,)), dma((n_chord,)), dma((n_chord,)), dma((4,)), dma((4,)),
                dma((2, n_z)), dma((2, n_z)), dma((n_z,)), dma((n_z,)), dma((n_z,)), dma((n_z,)),
            ],
            compiler_params=pltpu.CompilerParams(
                collective_id=0, has_side_effects=True, vmem_limit_bytes=64 * 1024 * 1024),
            name="sweeps",
        )(
            rhs.reshape(comp, rows, width), jet_mask.reshape(rows, width), jet_source,
            wall_flags.reshape(2, lines, width), bc_table,
            flat(xi_lower), flat(xi_upper), halved(eta_lower), halved(eta_upper),
        )
        return out.reshape(comp, span, cells, width)

    placed = (
        P(None, None, "wall", "chord"),
        P(None, "wall", "chord"),
        P(),
        P(None, "chord"),
        P(),
        P(None, None, None, "wall", "chord"),
        P(None, None, None, "wall", "chord"),
        P(None, None, None, "wall", "chord"),
        P(None, None, None, "wall", "chord"),
    )
    return jax.shard_map(
        per_device, mesh=mesh, in_specs=placed,
        out_specs=P(None, None, "wall", "chord"), check_vma=False)
```

```python
import functools

import jax
import jax.numpy as jnp
from jax import lax
from jax.experimental import pallas as pl
from jax.experimental.pallas import tpu as pltpu
from jax.sharding import PartitionSpec as P

C = 5
ROWS = 8
PACK = 4


def shifted(x, step, fill_eye, reverse):
    a, m, rows, width = x.shape
    flat = x.reshape(a * m * rows, width)
    moved = pltpu.roll(flat, width - step if reverse else step, 1).reshape(x.shape)
    lane = lax.broadcasted_iota(jnp.int32, x.shape, 3)
    keep = lane < width - step if reverse else lane >= step
    row = lax.broadcasted_iota(jnp.int32, x.shape, 0)
    col = lax.broadcasted_iota(jnp.int32, x.shape, 1)
    fill = jnp.where(row == col, 1.0, 0.0).astype(jnp.float32)
    return jnp.where(keep, moved, fill)


def apply_blocks(left, right):
    total = left[:, 0:1] * right[0:1]
    for b in range(1, C):
        total = total + left[:, b : b + 1] * right[b : b + 1]
    return total


def compose(later, earlier):
    made = apply_blocks(later[:, :C], earlier)
    return jnp.concatenate([made[:, :C], made[:, C:] + later[:, C:]], axis=1)


def scan_lanes(both, reverse):
    step = PACK
    while step < both.shape[3]:
        both = compose(both, shifted(both, step, True, reverse))
        step *= 2
    return both


def roll2(x, by):
    width = x.shape[-1]
    return pltpu.roll(x.reshape(-1, width), by % width, 1).reshape(x.shape)


def interleave(parts):
    lane = lax.broadcasted_iota(jnp.int32, parts[0].shape, 2)
    for bit in (1, 2):
        odd = (lane & bit) != 0
        made = list(parts)
        for i in range(PACK):
            if i & bit == 0:
                lo, hi = parts[i], parts[i | bit]
                made[i] = jnp.where(odd, roll2(hi, bit), lo)
                made[i | bit] = jnp.where(odd, hi, roll2(lo, -bit))
        parts = made
    return parts


def kernel(
    n_chord, n_z, n_zo,
    rhs_h, mask_h, jet_h, flags_h, table_h, xl_h, xu_h, el_h, eu_h,
    out_h,
    rhs, mask, xl, xu, jet, flags_v, table, el, eu, prefix, summary, sol, sol_in, res,
    maps_out, maps_in, ends_out, ends_in, flow_out, flow_in, flow,
    load_sem, own_sem, chord_send, chord_recv, pair_send, pair_recv,
    maps_send, maps_recv, ends_send, ends_recv, flow_send, flow_recv,
):
    chord = lax.axis_index("chord")
    wall = lax.axis_index("wall")
    zi, core = wall // 2, lax.rem(wall, 2)
    other = 1 - core
    groups = rhs.shape[1] // ROWS
    half_groups = groups // 2
    lines = el.shape[2] // 2
    width = rhs.shape[2]
    kz = maps_out.shape[2]

    def when(own, cond_of):
        if n_zo == n_z:
            own()
        else:
            pl.when(cond_of)(own)

    loads = [
        pltpu.make_async_copy(h, v, load_sem.at[i])
        for i, (h, v) in enumerate(((xl_h, xl), (xu_h, xu), (rhs_h, rhs), (mask_h, mask),
                                   (jet_h, jet), (flags_h, flags_v), (table_h, table)))
    ]
    for c in loads:
        c.start()

    barrier = pltpu.get_barrier_semaphore()
    pl.semaphore_signal(barrier, inc=1, device_id=(chord, zi * 2 + other),
                        device_id_type=pl.DeviceIdType.MESH)
    for r in range(1, n_z):
        pl.semaphore_signal(barrier, inc=1, device_id=(chord, lax.rem(zi + r, n_z) * 2 + core),
                            device_id_type=pl.DeviceIdType.MESH)
    for r in range(1, n_chord):
        pl.semaphore_signal(barrier, inc=1, device_id=(lax.rem(chord + r, n_chord), wall),
                            device_id_type=pl.DeviceIdType.MESH)
    pl.semaphore_wait(barrier, n_z + n_chord - 1)

    def to_wall(src, dst, send, recv, peer):
        return pltpu.make_async_remote_copy(
            src_ref=src, dst_ref=dst, send_sem=send, recv_sem=recv,
            device_id=(chord, peer), device_id_type=pl.DeviceIdType.MESH)

    def to_core(i, src, dst):
        return to_wall(src, dst, pair_send.at[i], pair_recv.at[i], zi * 2 + other)

    def to_z(src, dst, send, recv, z):
        return to_wall(src, dst, send, recv, z * 2 + core)

    to_core(0, el_h.at[:, other], el.at[core]).start()
    to_core(1, eu_h.at[:, other], eu.at[core]).start()
    own_el = pltpu.make_async_copy(el_h.at[:, core], el.at[core], own_sem.at[0])
    own_eu = pltpu.make_async_copy(eu_h.at[:, core], eu.at[core], own_sem.at[1])
    own_el.start()
    own_eu.start()
    for i in (0, 2, 3, 4):
        loads[i].wait()

    def cell(ref, j):
        return ref[j // 2, :, pl.ds(j % 2, lines, stride=2), :]

    def block(ref, j):
        return cell(ref, j).reshape(C, C, lines, width)

    lane = lax.broadcasted_iota(jnp.int32, (ROWS, width), 1)

    def tile(ref, q):
        return ref[:, q * ROWS : (q + 1) * ROWS, :]

    def sources(q):
        hit = mask[q * ROWS : (q + 1) * ROWS, :].astype(jnp.float32)
        x = tile(rhs, q)
        return jnp.stack([x[c] + hit * jet[c] for c in range(C)])

    source = interleave([sources(q) for q in range(PACK)])
    lower = interleave([tile(xl, q) for q in range(PACK)])
    runs = []
    for t in range(PACK):
        x = jnp.concatenate([lower[t].reshape(C, C, ROWS, width), source[t][:, None]], axis=1)
        runs.append(compose(x, runs[-1]) if runs else x)
    last = scan_lanes(runs[PACK - 1], False)
    before = shifted(last, PACK, True, False)
    full = [compose(runs[t], before) for t in range(PACK - 1)] + [last]
    loads[1].wait()
    upper = interleave([tile(xu, q) for q in range(PACK)])
    runs = [None] * PACK
    for t in range(PACK - 1, -1, -1):
        x = jnp.concatenate([upper[t].reshape(C, C, ROWS, width), full[t]], axis=1)
        runs[t] = compose(x, runs[t + 1]) if t < PACK - 1 else x
    first = scan_lanes(runs[0], True)
    before = shifted(first, PACK, True, True)
    packs = [jnp.zeros((ROWS, width), jnp.float32) for _ in range(summary.shape[1])]
    fields = [(last[a, m], PACK - width) for a in range(C) for m in range(6)]
    fields += [(first[a, m], 0) for a in range(C) for m in range(11)]
    per = width // PACK
    for i, (x, base) in enumerate(fields):
        at = PACK * (i % per)
        packs[i // per] = jnp.where((lane >= at) & (lane < at + PACK), roll2(x, at + base), packs[i // per])
    for i, x in enumerate(packs):
        summary[chord, i] = x

    def to_chord(r, slot):
        return pltpu.make_async_remote_copy(
            src_ref=summary.at[slot], dst_ref=summary.at[slot],
            send_sem=chord_send.at[r], recv_sem=chord_recv.at[r],
            device_id=(lax.rem(chord + r, n_chord), wall), device_id_type=pl.DeviceIdType.MESH)

    for r in range(1, n_chord):
        to_chord(r, chord).start()

    own_el.wait()
    own_eu.wait()
    to_core(0, el_h.at[:, 0], el.at[other]).wait_recv()
    to_core(1, eu_h.at[:, 0], eu.at[other]).wait_recv()
    reach = [block(el, 0)]
    for j in range(1, 4):
        reach.append(apply_blocks(block(el, j), reach[-1]))
    back, through = reach[3], block(eu, 3)
    for j in (2, 1, 0):
        blocks = block(eu, j)
        back = apply_blocks(blocks, back) + reach[j]
        through = apply_blocks(blocks, through)
    for i, m in enumerate((back, reach[3], through)):
        m = m.reshape(C * C, lines, width)
        for o in range(n_zo):
            maps_out[o, i * 25 : (i + 1) * 25] = m[:, o * kz : (o + 1) * kz]

    def scatter(src, dst, send, recv):
        for r in range(1, n_z):
            z = lax.rem(zi + r, n_z)
            when(lambda r=r, z=z: to_z(src.at[z], dst.at[zi], send.at[r], recv.at[r], z).start(), z < n_zo)

    def scatter_own(src, dst, sem):
        return pltpu.make_async_copy(src.at[zi], dst.at[zi], sem)

    def scatter_sent(src, dst, send, recv):
        for r in range(1, n_z):
            z = lax.rem(zi + r, n_z)
            when(lambda r=r, z=z: to_z(src.at[z], dst.at[zi], send.at[r], recv.at[r], z).wait_send(), z < n_zo)

    def scattered(src, dst, send, recv):
        for r in range(1, n_z):
            z = lax.rem(zi + n_z - r, n_z)
            to_z(src.at[0], dst.at[z], send.at[r], recv.at[r], z).wait_recv()

    owner = zi < n_zo
    def map_copies(z_out, z_in, r, to):
        return [
            to_z(maps_out.at[z_out, part], maps_in.at[z_in, part], maps_send.at[i, r], maps_recv.at[i, r], to)
            for i, part in enumerate((pl.ds(0, C * C), pl.ds(C * C, 2 * C * C)))
        ]

    def each_map(act, copies, sender, condition):
        turn, inner = sender > 0, (sender > 0) & (sender < n_z - 1)
        if condition is not None:
            turn, inner = turn & condition, inner & condition
        pl.when(turn)(lambda: act(copies[0]))
        pl.when(inner)(lambda: act(copies[1]))

    def maps_outward(act):
        for r in range(1, n_z):
            z = lax.rem(zi + r, n_z)
            each_map(act, map_copies(z, zi, r, z), zi, None if n_zo == n_z else z < n_zo)

    maps_outward(lambda c: c.start())
    when(lambda: scatter_own(maps_out, maps_in, own_sem.at[2]).start(), owner)
    prefix[0] = first.reshape(C * 11, ROWS, width)
    for t in range(1, PACK):
        prefix[t] = compose(runs[t], before).reshape(C * 11, ROWS, width)
    for r in range(1, n_chord):
        to_chord(r, lax.rem(chord + n_chord - r, n_chord)).wait_recv()


    def field(d, i):
        return roll2(summary[d, i // per], -PACK * (i % per))

    zero = jnp.zeros((ROWS, width), jnp.float32)
    ins = [[zero] * C]
    for d in range(n_chord - 1):
        made = []
        for a in range(C):
            t = field(d, a * 6 + 5)
            if d > 0:
                for b in range(C):
                    t = t + field(d, a * 6 + b) * ins[d][b]
            made.append(t)
        ins.append(made)
    backs = [None] * n_chord
    backs[n_chord - 1] = [zero] * C
    for d in range(n_chord - 1, 0, -1):
        made = []
        for a in range(C):
            base = 30 + a * 11
            t = field(d, base + 10)
            for b in range(C):
                t = t + field(d, base + 5 + b) * ins[d][b]
            if d < n_chord - 1:
                for b in range(C):
                    t = t + field(d, base + b) * backs[d][b]
            made.append(t)
        backs[d - 1] = made
    mine_in, mine_back = ins[0], backs[0]
    for d in range(1, n_chord):
        mine_in = [jnp.where(chord == d, x, y) for x, y in zip(ins[d], mine_in)]
        mine_back = [jnp.where(chord == d, x, y) for x, y in zip(backs[d], mine_back)]
    inflow = jnp.where(lane[None] < PACK, jnp.stack(mine_in + mine_back), 0.0)
    by = PACK
    while by < width:
        inflow = inflow + roll2(inflow, by)
        by *= 2
    behind = []
    for t in range(PACK):
        x = prefix[t].reshape(C, 11, ROWS, width)
        total = x[:, 10]
        for b in range(C):
            total = total + x[:, 5 + b] * inflow[b] + x[:, b] * inflow[C + b]
        behind.append(total)
    for q, x in enumerate(interleave(behind)):
        at = (q % half_groups) * ROWS
        sol[q // half_groups, :, at : at + ROWS, :] = x

    to_core(2, sol.at[other], sol_in.at[core]).start()
    own_sol = pltpu.make_async_copy(sol.at[core], sol_in.at[core], own_sem.at[3])
    own_sol.start()
    loads[5].wait()
    loads[6].wait()
    kind = flags_v[core]
    factor = []
    for c in range(C):
        t = jnp.zeros(kind.shape, jnp.float32)
        for f in range(table.shape[0]):
            t = jnp.where(kind == f, table[f, c], t)
        factor.append(jnp.where(zi == 0, t, 1.0))
    factor = jnp.stack(factor)
    own_sol.wait()
    to_core(2, sol.at[0], sol_in.at[other]).wait_recv()

    def value(j):
        return cell(sol_in, j) * factor if j == 0 else cell(sol_in, j)

    def step(ref, j, state):
        return apply_blocks(block(ref, j), state[:, None])[:, 0]

    lifted = [value(0)]
    for j in range(1, 4):
        lifted.append(value(j) + step(el, j, lifted[-1]))
    first = lifted[3]
    for j in (2, 1, 0):
        first = lifted[j] + step(eu, j, first)
    for o in range(n_zo):
        ends_out[o, :C] = lifted[3][:, o * kz : (o + 1) * kz]
        ends_out[o, C:] = first[:, o * kz : (o + 1) * kz]
    scatter(ends_out, ends_in, ends_send, ends_recv)
    when(lambda: scatter_own(ends_out, ends_in, own_sem.at[4]).start(), owner)

    def own_lines():
        scatter_own(maps_out, maps_in, own_sem.at[2]).wait()
        for r in range(1, n_z):
            z = lax.rem(zi + n_z - r, n_z)
            each_map(lambda c: c.wait_recv(), map_copies(0, z, r, z), z, None)
        scatter_own(ends_out, ends_in, own_sem.at[4]).wait()
        scattered(ends_out, ends_in, ends_send, ends_recv)

        def through_map(z, i, state):
            m = maps_in[z, i * 25 : (i + 1) * 25].reshape(C, C, kz, width)
            return apply_blocks(m, state[:, None])[:, 0]

        zero = jnp.zeros((C, kz, width), jnp.float32)
        ins = [zero, ends_in[0, :C]]
        for z in range(1, n_z - 1):
            ins.append(ends_in[z, :C] + through_map(z, 1, ins[-1]))
        backs = [zero]
        for z in range(n_z - 1, 0, -1):
            t = ends_in[z, C:] + through_map(z, 0, ins[z])
            if z < n_z - 1:
                t = t + through_map(z, 2, backs[-1])
            backs.append(t)
        backs = backs[::-1]
        for z in range(n_z):
            flow_out[z, :C] = ins[z]
            flow_out[z, C:] = backs[z]
        for r in range(1, n_z):
            z = lax.rem(zi + r, n_z)
            to_z(flow_out.at[z], flow_in.at[zi], flow_send.at[r], flow_recv.at[r], z).start()
        scatter_own(flow_out, flow_in, own_sem.at[5]).start()

    when(own_lines, owner)
    when(lambda: scatter_own(flow_out, flow_in, own_sem.at[5]).wait(), owner)
    for r in range(1, n_z):
        z = lax.rem(zi + n_z - r, n_z)
        when(lambda r=r, z=z: to_z(flow_out.at[0], flow_in.at[z], flow_send.at[r], flow_recv.at[r], z).wait_recv(),
             z < n_zo)
    for o in range(n_zo):
        flow[:, o * kz : (o + 1) * kz] = flow_in[o]

    def ship(half):
        @pl.when(core == half)
        def _():
            pltpu.make_async_copy(res.at[half], out_h.at[:, half], own_sem.at[6]).start()

        @pl.when(core != half)
        def _():
            to_core(3, res.at[half], out_h.at[:, core]).start()

    state = flow[:C]
    lifted = []
    for j in range(4):
        state = value(j) + step(el, j, state)
        lifted.append(state)
    state = flow[C:]
    for j in (3, 2, 1, 0):
        state = lifted[j] + step(eu, j, state)
        res[j // 2, :, pl.ds(j % 2, lines, stride=2), :] = state
        if j % 2 == 0:
            ship(j // 2)

    for i, src, dst in ((0, el_h.at[:, other], el.at[core]), (1, eu_h.at[:, other], eu.at[core]),
                        (2, sol.at[other], sol_in.at[core]), (3, res.at[other], out_h.at[:, core])):
        to_core(i, src, dst).wait_send()
    maps_outward(lambda c: c.wait_send())
    scatter_sent(ends_out, ends_in, ends_send, ends_recv)

    def flow_sent():
        for r in range(1, n_z):
            z = lax.rem(zi + r, n_z)
            to_z(flow_out.at[z], flow_in.at[zi], flow_send.at[r], flow_recv.at[r], z).wait_send()

    when(flow_sent, owner)
    for r in range(1, n_chord):
        to_chord(r, chord).wait_send()
    pltpu.make_async_copy(res.at[core], out_h.at[:, core], own_sem.at[6]).wait()
    to_core(3, res.at[0], out_h.at[:, other]).wait_recv()


def solution(mesh):
    n_chord, n_wall = mesh.shape["chord"], mesh.shape["wall"]

    def per_device(rhs, jet_mask, jet_source, wall_flags, bc_table,
                   xi_lower, xi_upper, eta_lower, eta_upper):
        comp, span, cells, width = rhs.shape
        n_z = n_wall // 2
        lines = span // 2
        n_zo = min(n_z, lines)
        kz = lines // n_zo
        rows = span * cells
        half = rows // 2
        flat = lambda x: x.reshape(comp * comp, rows, width)
        halved = lambda x: x.reshape(comp * comp, 2, half, width)
        hbm = pl.BlockSpec(memory_space=pltpu.HBM)
        f32 = jnp.float32
        dma = pltpu.SemaphoreType.DMA
        out = pl.pallas_call(
            functools.partial(kernel, n_chord, n_z, n_zo),
            out_shape=jax.ShapeDtypeStruct((comp, 2, half, width), f32),
            in_specs=[hbm] * 9,
            out_specs=hbm,
            scratch_shapes=[
                pltpu.VMEM((comp, rows, width), f32),
                pltpu.VMEM((rows, width), jnp.int32),
                pltpu.VMEM((comp * comp, rows, width), f32),
                pltpu.VMEM((comp * comp, rows, width), f32),
                pltpu.SMEM(jet_source.shape, f32),
                pltpu.VMEM((2, lines, width), jnp.int32),
                pltpu.SMEM(bc_table.shape, f32),
                pltpu.VMEM((2, comp * comp, half, width), f32),
                pltpu.VMEM((2, comp * comp, half, width), f32),
                pltpu.VMEM((PACK, comp * 11, ROWS, width), f32),
                pltpu.VMEM((n_chord, -(-85 * PACK // width), ROWS, width), f32),
                pltpu.VMEM((2, comp, half, width), f32),
                pltpu.VMEM((2, comp, half, width), f32),
                pltpu.VMEM((2, comp, half, width), f32),
                pltpu.VMEM((n_zo, 3 * comp * comp, kz, width), f32),
                pltpu.VMEM((n_z, 3 * comp * comp, kz, width), f32),
                pltpu.VMEM((n_zo, 2 * comp, kz, width), f32),
                pltpu.VMEM((n_z, 2 * comp, kz, width), f32),
                pltpu.VMEM((n_z, 2 * comp, kz, width), f32),
                pltpu.VMEM((n_zo, 2 * comp, kz, width), f32),
                pltpu.VMEM((2 * comp, lines, width), f32),
                dma((7,)), dma((7,)), dma((n_chord,)), dma((n_chord,)), dma((4,)), dma((4,)),
                dma((2, n_z)), dma((2, n_z)), dma((n_z,)), dma((n_z,)), dma((n_z,)), dma((n_z,)),
            ],
            compiler_params=pltpu.CompilerParams(
                collective_id=0, has_side_effects=True, vmem_limit_bytes=64 * 1024 * 1024),
            name="sweeps",
        )(
            rhs.reshape(comp, rows, width), jet_mask.reshape(rows, width), jet_source,
            wall_flags.reshape(2, lines, width), bc_table,
            flat(xi_lower), flat(xi_upper), halved(eta_lower), halved(eta_upper),
        )
        return out.reshape(comp, span, cells, width)

    placed = (
        P(None, None, "wall", "chord"),
        P(None, "wall", "chord"),
        P(),
        P(None, "chord"),
        P(),
        P(None, None, None, "wall", "chord"),
        P(None, None, None, "wall", "chord"),
        P(None, None, None, "wall", "chord"),
        P(None, None, None, "wall", "chord"),
    )
    return jax.shard_map(
        per_device, mesh=mesh, in_specs=placed,
        out_specs=P(None, None, "wall", "chord"), check_vma=False)
```
